256 devices in a mesh: pop: 8 (over z), seq: 32 (over y, x, core).
Axes of the slice: x: 4, y: 4, z: 8, core: 2. Of those that a mesh axis runs over, the one named last changes fastest.
Arguments:
- queries: bfloat16 [16384, 2048], P(('pop', 'seq')), parts along dimension 0, may hold values from -12 to 12
- keys: bfloat16 [131072, 2048], P(('pop', 'seq')), parts along dimension 0, may hold values from -4 to 4
- values: bfloat16 [131072, 2048], P(('pop', 'seq')), parts along dimension 0, may hold values from -6 to 6
- cotangent: bfloat16 [16384, 2048], P(('pop', 'seq')), parts along dimension 0, may hold values from -6 to 6
- neighbour_ids: int32 [256, 8], P('pop'), parts along dimension 0, may hold values from 0 to 127, as said below
- neighbour_counts: int32 [256], P('pop'), parts along dimension 0, may hold values from 2 to 8
Outputs:
- attended: bfloat16 [16384, 2048], P(('pop', 'seq')), parts along dimension 0
- query_grad: bfloat16 [16384, 2048], P(('pop', 'seq')), parts along dimension 0
- key_grad: bfloat16 [131072, 2048], P(('pop', 'seq')), parts along dimension 0
- value_grad: bfloat16 [131072, 2048], P(('pop', 'seq')), parts along dimension 0
The draws below stay inside these ranges and needn't reach their ends.
There are 8 independent parts, one for each index of `pop`. The reference program is written for one: setup_inputs(seed, part) draws one part's arguments, and reference() takes and returns one part's arrays. A program takes and returns all parts, laid end to end along the dimension named above; each array names one. Nothing has to cross between parts.
Inputs may be any that keep to these rules, and one draw needn't show every extreme that they name: `neighbour_ids`: the entries of one group's list are distinct; each names a neighbour held by the index of seq that holds the group or by the next index, the last index's next being index 0 (neighbour n is held by index n // 4, group c by index c); entries at or past the group's count are ignored.
All inputs are finite; a program needn't handle non-finite values.
Results may differ from the reference program's by a relative error of at most 0.04.
Values may be sent and summed in bfloat16 or wider, within the bound.
No kernel may reach another device: no remote copies, remote signals or barrier semaphores. Data moves between devices by JAX's collectives and lax.ppermute only.
A program may use at most 128 MiB of HBM per device.

```python
import math
import jax
import jax.numpy as jnp
from jax import lax

HEADS = 16
HD = 128
GROUP = 64
NLEN = 128
SLOTS = 8
NB_DEV = 4
TOK_DEV = 64
TOKENS = 2048
GROUPS = 32
NEIGH = 128
NROWS = 16384


def neighbour_table(key):
    parts = jax.random.split(key, 7)
    per_device = TOK_DEV // GROUP
    holders = NEIGH // NB_DEV
    group = jnp.arange(GROUPS, dtype=jnp.int32)
    owner = group // per_device
    following = (owner + 1) % holders
    first = jax.random.randint(parts[0], (GROUPS,), 0, SLOTS - 1)
    second = jax.random.randint(parts[1], (GROUPS,), 0, SLOTS - 1)
    counts = 2 + jnp.minimum(first, second)
    biggest = jax.random.randint(parts[2], (), 0, GROUPS)
    smallest = (biggest + 1 + jax.random.randint(parts[3], (), 0, GROUPS - 1)) % GROUPS
    counts = jnp.where(group == biggest, SLOTS, counts)
    counts = jnp.where(group == smallest, 2, counts)
    pool = jnp.arange(NEIGH, dtype=jnp.int32)
    holder = pool // NB_DEV
    near = (holder[None, :] == owner[:, None]) | (holder[None, :] == following[:, None])
    raw = jax.random.randint(parts[4], (GROUPS, NEIGH), 1, 1 << 14)
    score = jnp.where(near, raw, 0)
    own_pick = owner * NB_DEV + jax.random.randint(parts[5], (GROUPS,), 0, NB_DEV)
    next_pick = following * NB_DEV + jax.random.randint(parts[6], (GROUPS,), 0, NB_DEV)
    score = jnp.where(pool[None, :] == own_pick[:, None], 1 << 15, score)
    score = jnp.where(pool[None, :] == next_pick[:, None], 1 << 15, score)
    distinct = score * NEIGH + pool[None, :]
    chosen = lax.top_k(distinct, SLOTS)[1].astype(jnp.int32)
    return (chosen, counts.astype(jnp.int32))


def draw_neighbour_ids(key, part):
    chosen, counts = neighbour_table(key)
    return chosen


def draw_neighbour_counts(key, part):
    chosen, counts = neighbour_table(key)
    return counts


def draw_queries(key, part):
    key = jax.random.fold_in(key, 3)
    base_key = jax.random.fold_in(key, 0)
    base = jnp.clip(jax.random.normal(base_key, (TOKENS, HEADS * HD)), -6.0, 6.0)
    return base.astype(jnp.bfloat16)


def draw_keys(key, part):
    key = jax.random.fold_in(key, 4)
    base = jnp.clip(jax.random.normal(key, (NROWS, HEADS * HD)), -4.0, 4.0)
    return base.astype(jnp.bfloat16)


def levels(own_key, dims, pieces, low, high):
    level, own = 1.0, jax.random.fold_in(own_key, 6)
    for dim, blocks in pieces:
        heights = jnp.exp(jax.random.uniform(jax.random.fold_in(own, dim), (blocks,), jnp.float32, low / len(pieces), high / len(pieces)))
        level = level * jnp.repeat(heights, dims[dim] // blocks).reshape([-1 if axis == dim else 1 for axis in range(len(dims))])
    return level


def bell_draw(rng, dims, scale, bound, shards=(), held_as=jnp.bfloat16):
    factor_of = levels(rng, dims, shards, -0.22, 0.18) if shards else 1.0
    values = jax.random.normal(rng, dims, jnp.float32) * scale * factor_of
    return jnp.minimum(jnp.maximum(values, -bound), bound).astype(held_as)


def setup_inputs(seed: int = 0, part: int = 0) -> dict:
    key_list = jax.random.split(jax.random.key(seed), 7)
    own_keys = jax.random.split(jax.random.fold_in(key_list[6], part), 7)
    queries = draw_queries(jax.random.fold_in(jax.random.fold_in(key_list[6], part), 71), part)
    keys = draw_keys(jax.random.fold_in(jax.random.fold_in(key_list[6], part), 71), part)
    values = bell_draw(own_keys[2], (NROWS, HEADS * HD), 1.0, 6.0, ((0, 32),))
    cotangent = bell_draw(own_keys[3], (TOKENS, HEADS * HD), 1.0, 6.0, ((0, 32),))
    neighbour_ids = draw_neighbour_ids(jax.random.fold_in(jax.random.fold_in(key_list[6], part), 71), part)
    neighbour_counts = draw_neighbour_counts(jax.random.fold_in(jax.random.fold_in(key_list[6], part), 71), part)
    return {"queries": queries, "keys": keys, "values": values, "cotangent": cotangent, "neighbour_ids": neighbour_ids, "neighbour_counts": neighbour_counts}


masked_low = -1e+30

def reference(queries, keys, values, cotangent, neighbour_ids, neighbour_counts):
    scale = 1.0 / math.sqrt(HD)
    key_pool = keys.reshape(NEIGH, NLEN, HEADS, HD)
    value_pool = values.reshape(NEIGH, NLEN, HEADS, HD)
    query_groups = queries.reshape(GROUPS, GROUP, HEADS, HD)
    grad_groups = cotangent.reshape(GROUPS, GROUP, HEADS, HD)

    def step(carry, item):
        key_acc, value_acc = carry
        query_rows, grad_rows, group_ids, group_count = item
        key_rows = jnp.take(key_pool, group_ids, axis=0).astype(jnp.float32)
        value_rows = jnp.take(value_pool, group_ids, axis=0).astype(jnp.float32)
        query_f = query_rows.astype(jnp.float32)
        grad_f = grad_rows.astype(jnp.float32)
        live = jnp.arange(SLOTS, dtype=jnp.int32) < group_count
        block = group_ids // NB_DEV
        keep = live[None, None, :, None]
        scores = jnp.einsum('ihd,snhd->hisn', query_f, key_rows) * scale
        scores = jnp.where(keep, scores, masked_low)
        slot_peak = lax.optimization_barrier(jnp.max(scores, axis=-1))
        same = (block[:, None] == block[None, :]) & live[None, :]
        peaks = lax.optimization_barrier(jnp.max(jnp.where(same[None, None], slot_peak[:, :, None, :], masked_low), axis=-1))
        weights = jnp.where(keep, jnp.exp(scores - peaks[..., None]), 0.0)
        rounded = lax.optimization_barrier(weights.astype(jnp.bfloat16)).astype(jnp.float32)
        numer = jnp.einsum('hisn,snhd->hisd', rounded, value_rows)
        totals = lax.optimization_barrier(jnp.sum(weights, axis=-1))
        top = lax.optimization_barrier(jnp.max(jnp.where(live, peaks, masked_low), axis=-1))
        factor = jnp.where(live, jnp.exp(jnp.where(live, peaks - top[..., None], masked_low)), 0.0)
        denom = lax.optimization_barrier(jnp.sum(factor * totals, axis=-1))
        attended = lax.optimization_barrier(jnp.sum(factor[..., None] * numer, axis=2)) / denom[..., None]
        output = jnp.transpose(attended, (1, 0, 2)).astype(jnp.bfloat16)
        lse = top + jnp.log(denom)
        prob = jnp.where(keep, jnp.exp(scores - lse[..., None, None]), 0.0)
        prob_round = lax.optimization_barrier(prob.astype(jnp.bfloat16)).astype(jnp.float32)
        value_term = jnp.einsum('hisn,ihd->snhd', prob_round, grad_f)
        dprob = jnp.einsum('ihd,snhd->hisn', grad_f, value_rows)
        delta = jnp.transpose(lax.optimization_barrier(jnp.sum(grad_f * output.astype(jnp.float32), axis=-1)), (1, 0))
        dscore = prob * (dprob - delta[..., None, None])
        dscore = lax.optimization_barrier(dscore.astype(jnp.bfloat16)).astype(jnp.float32)
        query_term = (jnp.einsum('hisn,snhd->ihd', dscore, key_rows) * scale).astype(jnp.bfloat16)
        key_term = jnp.einsum('hisn,ihd->snhd', dscore, query_f) * scale
        key_acc = key_acc.at[group_ids].add(key_term)
        value_acc = value_acc.at[group_ids].add(value_term)
        return ((key_acc, value_acc), (output, query_term))
    empty = jnp.zeros((NEIGH, NLEN, HEADS, HD), jnp.float32)
    (key_acc, value_acc), (outputs, query_terms) = lax.scan(step, (empty, empty), (query_groups, grad_groups, neighbour_ids, neighbour_counts))
    attended = outputs.reshape(TOKENS, HEADS * HD)
    query_grad = query_terms.reshape(TOKENS, HEADS * HD)
    key_grad = key_acc.reshape(NROWS, HEADS * HD).astype(jnp.bfloat16)
    value_grad = value_acc.reshape(NROWS, HEADS * HD).astype(jnp.bfloat16)
    return (attended, query_grad, key_grad, value_grad)
```

```python
import functools
import math

import jax
import jax.numpy as jnp
from jax import lax
from jax.experimental import pallas as pl
from jax.experimental.pallas import tpu as pltpu
from jax.sharding import PartitionSpec as P

HD = 128
GROUP = 64
NLEN = 128
SLOTS = 8
PAIR = 2 * HD
SCALE = 1.0 / math.sqrt(HD)
TO_LOG2 = SCALE / math.log(2.0)
DEAD = -1e30
WIDE = 512
BF16 = jnp.bfloat16
F32 = jnp.float32
NT = (((1,), (1,)), ((), ()))
NN = (((1,), (0,)), ((), ()))
TN = (((0,), (0,)), ((), ()))


def dot(a, b, dims):
    return lax.dot_general(a, b, dims, preferred_element_type=F32)


def two_heads(x):
    zero = jnp.zeros((GROUP, HD), x.dtype)
    first = jnp.concatenate([x[:, :HD], zero], 1)
    second = jnp.concatenate([zero, x[:, HD:]], 1)
    return jnp.concatenate([first, second], 0)


def own_columns(x):
    return jnp.concatenate([x[:GROUP, :HD], x[GROUP:, HD:]], 1)


def column(row):
    tall = jnp.transpose(jnp.broadcast_to(row, (HD, 2 * GROUP)))
    return jnp.concatenate([tall[:GROUP], tall[GROUP:]], 1)


def live_bias(ids, counts, group, first):
    out = []
    for n in range(4):
        hit = jnp.int32(0)
        for j in range(SLOTS):
            match = (ids[group, j] == first + n) & (j < counts[group])
            hit = hit | match.astype(jnp.int32)
        out.append(jnp.where(hit > 0, F32(0.0), F32(DEAD)))
    return out


def softmax_part(k, qb, bias):
    raw = dot(k, qb, NT)
    s = jnp.concatenate([raw[n * NLEN : (n + 1) * NLEN] * TO_LOG2 + bias[n] for n in range(4)], 0)
    peak = jnp.max(s, axis=0, keepdims=True)
    e = jnp.exp2(s - peak)
    total = jnp.sum(e, axis=0, keepdims=True)
    return (e, peak + jnp.log2(total), total)


def own_forward(ids, counts, q, g, k, v, stats, att, weights, dprob):
    step = pl.program_id(0)
    index = lax.axis_index("seq")
    bias = live_bias(ids, counts, index, index * 4)
    for u in range(WIDE // PAIR):
        c = slice(u * PAIR, (u + 1) * PAIR)
        h = slice(u * HD, (u + 1) * HD)
        vv = v[:, c]
        e, lse, total = softmax_part(k[:, c], two_heads(q[:, c]), bias)
        inv = 1.0 / total
        dp = dot(vv, two_heads(g[:, c]), NT)
        row = step * (WIDE // PAIR) + u
        stats[pl.ds(row, 1), :] = lse
        stats[pl.ds(row + 8, 1), :] = jnp.sum(e * dp, axis=0, keepdims=True) * inv
        att[:, c] = own_columns(dot(e.astype(BF16), vv, TN)) * column(inv)
        weights[:, h] = (e * inv).astype(BF16)
        dprob[:, h] = dp.astype(BF16)


def far_forward(ids, counts, q, k, v, lse_out, att, weights):
    step = pl.program_id(0)
    index = lax.axis_index("seq")
    holders = lax.axis_size("seq")
    group = lax.rem(index + holders - 1, holders)
    bias = live_bias(ids, counts, group, index * 4)
    for u in range(WIDE // PAIR):
        c = slice(u * PAIR, (u + 1) * PAIR)
        h = slice(u * HD, (u + 1) * HD)
        e, lse, total = softmax_part(k[:, c], two_heads(q[:, c]), bias)
        inv = 1.0 / total
        row = step * (WIDE // PAIR) + u
        lse_out[pl.ds(row, 1), :] = lse
        att[:, c] = (own_columns(dot(e.astype(BF16), v[:, c], TN)) * column(inv)).astype(BF16)
        weights[:, h] = (e * inv).astype(BF16)


def merged(lse_a, lse_b):
    top = jnp.maximum(lse_a, lse_b)
    a = jnp.exp2(lse_a - top)
    b = jnp.exp2(lse_b - top)
    inv = 1.0 / (a + b)
    return (a * inv, b * inv)


def far_backward(g, k, v, weights, lse_far, stats_own, dq, prob, dscore):
    step = pl.program_id(0)
    for u in range(WIDE // PAIR):
        c = slice(u * PAIR, (u + 1) * PAIR)
        h = slice(u * HD, (u + 1) * HD)
        row = step * (WIDE // PAIR) + u
        share_own, share_far = merged(stats_own[pl.ds(row, 1), :], lse_far[pl.ds(row, 1), :])
        w = weights[:, h].astype(F32)
        dp = dot(v[:, c], two_heads(g[:, c]), NT)
        delta = share_own * stats_own[pl.ds(row + 8, 1), :] + share_far * jnp.sum(
            w * dp, axis=0, keepdims=True
        )
        p = w * share_far
        ds = (p * (dp - delta)).astype(BF16)
        dq[:, c] = (own_columns(dot(ds, k[:, c], TN)) * SCALE).astype(BF16)
        prob[:, h] = p.astype(BF16)
        dscore[:, h] = ds


def finish(
    q, g, q_far, g_far, k, w_own, dp_own, p_far, ds_far, att_own, att_far, stats, lse_far,
    out, dq, dk, dv,
):
    step = pl.program_id(0)
    for u in range(WIDE // PAIR):
        c = slice(u * PAIR, (u + 1) * PAIR)
        h = slice(u * HD, (u + 1) * HD)
        row = step * (WIDE // PAIR) + u
        share_own, share_far = merged(stats[pl.ds(row, 1), :], lse_far[pl.ds(row, 1), :])
        attended = (
            att_own[:, c] * column(share_own) + att_far[:, c].astype(F32) * column(share_far)
        ).astype(BF16)
        out[:, c] = attended
        gg = g[:, c]
        prod = gg.astype(F32) * attended.astype(F32)
        tall = jnp.concatenate([prod[:, :HD], prod[:, HD:]], 0)
        delta = jnp.sum(jnp.transpose(tall), axis=0, keepdims=True)
        p = w_own[:, h].astype(F32) * share_own
        ds = (p * (dp_own[:, h].astype(F32) - delta)).astype(BF16)
        qb = two_heads(q[:, c])
        dq[:, c] = own_columns(dot(ds, k[:, c], TN)) * SCALE
        p_all = jnp.concatenate([p.astype(BF16), p_far[:, h]], 1)
        ds_all = jnp.concatenate([ds, ds_far[:, h]], 1)
        g_all = jnp.concatenate([two_heads(gg), two_heads(g_far[:, c])], 0)
        q_all = jnp.concatenate([qb, two_heads(q_far[:, c])], 0)
        dv[:, c] = dot(p_all, g_all, NN).astype(BF16)
        dk[:, c] = (dot(ds_all, q_all, NN) * SCALE).astype(BF16)


def passed_along(block, distance):
    count = lax.axis_size("seq")
    route = [((i - distance) % count, i) for i in range(count)]
    return lax.ppermute(block, "seq", route)


def call(body, name, ins, outs, flops):
    def spec(kind, rows):
        if kind == "scalar":
            return pl.BlockSpec(memory_space=pltpu.SMEM)
        if kind == "wide":
            return pl.BlockSpec((rows, WIDE), lambda i: (0, i))
        if kind == "half":
            return pl.BlockSpec((rows, WIDE // 2), lambda i: (0, i))
        return pl.BlockSpec((rows, HD), lambda i: (0, 0))

    width = {"wide": 2048, "half": 1024, "rows": HD}
    shapes = [jax.ShapeDtypeStruct((r, width[kind]), t) for kind, r, t in outs]
    return pl.pallas_call(
        body,
        grid=(2048 // WIDE,),
        in_specs=[spec(kind, x.shape[0]) for kind, x in ins],
        out_specs=[spec(kind, r) for kind, r, t in outs],
        out_shape=shapes,
        compiler_params=pltpu.CompilerParams(vmem_limit_bytes=32 << 20),
        cost_estimate=pl.CostEstimate(
            flops=flops, bytes_accessed=4 << 20, transcendentals=0
        ),
        name=name,
    )(*[x for kind, x in ins])


def per_device(queries, keys, values, cotangent, neighbour_ids, neighbour_counts):
    q_far = passed_along(queries, 1)
    g_far = passed_along(cotangent, 1)
    rows = keys.shape[0]
    ids = ("scalar", neighbour_ids)
    counts = ("scalar", neighbour_counts)
    q, g = ("wide", queries), ("wide", cotangent)
    k, v = ("wide", keys), ("wide", values)
    stats, att_own, w_own, dp_own = call(
        own_forward,
        "own_forward",
        [ids, counts, q, g, k, v],
        [("rows", 16, F32), ("wide", GROUP, F32), ("half", rows, BF16), ("half", rows, BF16)],
        1 << 30,
    )
    stats_in = passed_along(stats, 1)
    lse_far, att_far, w_far = call(
        far_forward,
        "far_forward",
        [ids, counts, ("wide", q_far), k, v],
        [("rows", 8, F32), ("wide", GROUP, BF16), ("half", rows, BF16)],
        1 << 30,
    )
    att_back = passed_along(att_far, -1)
    lse_back = passed_along(lse_far, -1)
    dq_far, p_far, ds_far = call(
        far_backward,
        "far_backward",
        [("wide", g_far), k, v, ("half", w_far), ("rows", lse_far), ("rows", stats_in)],
        [("wide", GROUP, BF16), ("half", rows, BF16), ("half", rows, BF16)],
        1 << 30,
    )
    dq_back = passed_along(dq_far, -1)
    out, dq_own, dk, dv = call(
        finish,
        "finish",
        [
            q, g, ("wide", q_far), ("wide", g_far), k, ("half", w_own), ("half", dp_own),
            ("half", p_far), ("half", ds_far), ("wide", att_own), ("wide", att_back),
            ("rows", stats), ("rows", lse_back),
        ],
        [("wide", GROUP, BF16), ("wide", GROUP, F32), ("wide", rows, BF16), ("wide", rows, BF16)],
        1 << 30,
    )
    query_grad = (dq_own + dq_back.astype(F32)).astype(BF16)
    return (out, query_grad, dk, dv)


def solution(mesh):
    split = P(("pop", "seq"), None)
    return jax.shard_map(
        per_device,
        mesh=mesh,
        in_specs=(split, split, split, split, P("pop", None), P("pop")),
        out_specs=(split, split, split, split),
        check_vma=False,
    )
```

```python
import math

import jax
import jax.numpy as jnp
from jax import lax
from jax.experimental import pallas as pl
from jax.experimental.pallas import tpu as pltpu
from jax.sharding import PartitionSpec as P

HD = 128
GROUP = 64
NLEN = 128
SLOTS = 8
HELD = 4
WIDTH = 2048
PAIR = 2 * HD
PAIRS = WIDTH // PAIR
ROWS = HELD * NLEN
SCALE = 1.0 / math.sqrt(HD)
TO_LOG2 = SCALE / math.log(2.0)
DEAD = -1e30
LOADS = (0, 2, 5, 8)
BF16 = jnp.bfloat16
F32 = jnp.float32
NT = (((1,), (1,)), ((), ()))
NN = (((1,), (0,)), ((), ()))
TN = (((0,), (0,)), ((), ()))
VMEM = pl.BlockSpec(memory_space=pltpu.VMEM)
HBM = pl.BlockSpec(memory_space=pltpu.HBM)


def dot(a, b, dims):
    return lax.dot_general(a, b, dims, preferred_element_type=F32)


def wide(p):
    return slice(p * PAIR, (p + 1) * PAIR)


def half(p):
    return slice(p * HD, (p + 1) * HD)


def two_heads(x):
    zero = jnp.zeros((GROUP, HD), x.dtype)
    first = jnp.concatenate([x[:, :HD], zero], 1)
    second = jnp.concatenate([zero, x[:, HD:]], 1)
    return jnp.concatenate([first, second], 0)


def own_columns(x):
    return jnp.concatenate([x[:GROUP, :HD], x[GROUP:, HD:]], 1)


def head_sums(x):
    tall = jnp.concatenate([x[:, :HD], x[:, HD:]], 0)
    return jnp.sum(jnp.transpose(tall), axis=0, keepdims=True)


def as_columns(rows):
    return jnp.transpose(jnp.concatenate([rows, jnp.zeros((HD - PAIRS, HD), F32)], 0))


def spread(columns, p):
    tall = jnp.broadcast_to(columns[:, p : p + 1], (2 * GROUP, HD))
    return jnp.concatenate([tall[:GROUP], tall[GROUP:]], 1)


def live_bias(ids, counts, group, first, n):
    hit = jnp.int32(0)
    for j in range(SLOTS):
        match = (ids[j, group] == first + n) & (j < counts[group])
        hit = hit | match.astype(jnp.int32)
    return jnp.where(hit > 0, F32(0.0), F32(DEAD))


def softmax_part(k, qb, bias):
    raw = dot(k, qb, NT)
    s = jnp.concatenate(
        [raw[n * NLEN : (n + 1) * NLEN] * TO_LOG2 + bias[n] for n in range(HELD)], 0
    )
    peak = jnp.max(s, axis=0, keepdims=True)
    e = jnp.exp2(s - peak)
    return (e.astype(BF16), peak, jnp.sum(e, axis=0, keepdims=True))


def merged(peak_a, total_a, peak_b, total_b):
    top = jnp.maximum(peak_a, peak_b)
    a = jnp.exp2(peak_a - top)
    b = jnp.exp2(peak_b - top)
    inv = 1.0 / (a * total_a + b * total_b)
    return (a * inv, b * inv)


def pieces(x, count):
    out = []
    for _ in range(count - 1):
        out.append(x.astype(BF16).astype(F32))
        x = x - out[-1]
    return out + [x]


def packed(figures):
    tall = []
    for rows, count in figures:
        tall += pieces(jnp.concatenate([rows[:, :GROUP], rows[:, GROUP:]], 0), count)
    tall = jnp.concatenate(tall + [jnp.zeros((HD - 16 * len(tall), GROUP), F32)], 0)
    tall = jnp.concatenate([tall, jnp.zeros((HD, GROUP), F32)], 1)
    return jnp.transpose(tall)[:GROUP].astype(BF16)


def unpacked(block, counts):
    tall = jnp.transpose(jnp.concatenate([block.astype(F32), jnp.zeros((GROUP, HD), F32)], 0))
    out, at = [], 0
    for count in counts:
        x = tall[at : at + 16]
        for n in range(1, count):
            x = x + tall[at + 16 * n : at + 16 * n + 16]
        out.append(jnp.concatenate([x[:PAIRS, :GROUP], x[PAIRS:, :GROUP]], 1))
        at += 16 * count
    return out


def own_forward(
    ids_hbm, counts_hbm, q_hbm, g_hbm, k_hbm, v_hbm,
    stats, numer, weights, dprob, bias_far, q, g, k, v,
    ids, counts, sems,
):
    copies = [
        pltpu.make_async_copy(ids_hbm, ids, sems.at[0]),
        pltpu.make_async_copy(counts_hbm, counts, sems.at[1]),
        pltpu.make_async_copy(q_hbm, q, sems.at[2]),
        pltpu.make_async_copy(g_hbm, g.at[:, :WIDTH], sems.at[3]),
    ]
    for n in range(len(LOADS) - 1):
        c = slice(LOADS[n] * PAIR, LOADS[n + 1] * PAIR)
        copies.append(pltpu.make_async_copy(k_hbm.at[:, c], k.at[:, c], sems.at[4 + 2 * n]))
        copies.append(pltpu.make_async_copy(v_hbm.at[:, c], v.at[:, c], sems.at[5 + 2 * n]))
    for copy in copies:
        copy.start()
    index = lax.axis_index("seq")
    before = lax.rem(index + lax.axis_size("seq") - 1, lax.axis_size("seq"))
    copies[0].wait()
    copies[1].wait()
    bias = [live_bias(ids, counts, index, index * HELD, n) for n in range(HELD)]
    for n in range(HELD):
        bias_far[n : n + 1, :] = jnp.full(
            (1, HD), live_bias(ids, counts, before, index * HELD, n), F32
        )
    bias_far[HELD:, :] = jnp.zeros((8 - HELD, HD), F32)
    copies[2].wait()
    copies[3].wait()
    for p in range(PAIRS):
        c, h = wide(p), half(p)
        if p in LOADS:
            n = LOADS.index(p)
            copies[4 + 2 * n].wait()
            copies[5 + 2 * n].wait()
        gg = g[:, c]
        e, peak, total = softmax_part(k[:, c], two_heads(q[:, c]), bias)
        part = own_columns(dot(e, v[:, c], TN))
        weights[:, h] = e
        numer[:, c] = part
        dprob[:, h] = dot(v[:, c], two_heads(gg), NT).astype(BF16)
        stats[p : p + 1, :] = peak
        stats[8 + p : 9 + p, :] = total
        stats[16 + p : 17 + p, :] = head_sums(part * gg.astype(F32))
    g[:, WIDTH:] = packed([(stats[:8, :], 3), (stats[8:16, :], 2), (stats[16:, :], 2)])


def far_forward(bias_ref, q, k, v, message, weights, stats):
    bias = [bias_ref[n : n + 1, :] for n in range(HELD)]
    for p in range(PAIRS):
        c, h = wide(p), half(p)
        e, peak, total = softmax_part(k[:, c], two_heads(q[:, c]), bias)
        message[:, c] = own_columns(dot(e, v[:, c], TN)).astype(BF16)
        weights[:, h] = e
        stats[p : p + 1, :] = peak
        stats[8 + p : 9 + p, :] = total
    message[:, WIDTH:] = packed([(stats[:8, :], 3), (stats[8:, :], 2)])


def far_backward(g, k, v, weights, message, stats, dq, prob, dscore):
    peak_own, total_own, dot_own = unpacked(g[:, WIDTH:], (3, 2, 2))
    own, far = merged(peak_own, total_own, stats[0:8, :], stats[8:16, :])
    delta_own = own * dot_own
    for p in range(PAIRS):
        c, h = wide(p), half(p)
        gg = g[:, c]
        row = slice(p, p + 1)
        delta = delta_own[row] + far[row] * head_sums(
            message[:, c].astype(F32) * gg.astype(F32)
        )
        dp = dot(v[:, c], two_heads(gg), NT)
        pr = weights[:, h].astype(F32) * far[row]
        ds = (pr * (dp - delta)).astype(BF16)
        dq[:, c] = (own_columns(dot(ds, k[:, c], TN)) * SCALE).astype(BF16)
        prob[:, h] = pr.astype(BF16)
        dscore[:, h] = ds


def finish(
    q, g, q_far, g_far, k, w_own, dp_own, p_far, ds_far, numer, message, stats,
    out_hbm, dq, dk_hbm, dv_hbm,
    out, dk, dv, sems,
):
    peak_far, total_far = unpacked(message[:, WIDTH:], (3, 2))
    own, far = merged(stats[0:8, :], stats[8:16, :], peak_far, total_far)
    own_tall, far_tall = as_columns(own), as_columns(far)
    copies = []
    for p in range(PAIRS):
        c, h = wide(p), half(p)
        row = slice(p, p + 1)
        gg = g[:, c]
        attended = (
            numer[:, c] * spread(own_tall, p) + message[:, c].astype(F32) * spread(far_tall, p)
        ).astype(BF16)
        out[:, c] = attended
        delta = head_sums(gg.astype(F32) * attended.astype(F32))
        pr = w_own[:, h].astype(F32) * own[row]
        ds = (pr * (dp_own[:, h].astype(F32) - delta)).astype(BF16)
        dq[:, c] = own_columns(dot(ds, k[:, c], TN)) * SCALE
        p_all = jnp.concatenate([pr.astype(BF16), p_far[:, h]], 1)
        ds_all = jnp.concatenate([ds, ds_far[:, h]], 1)
        g_all = jnp.concatenate([two_heads(gg), two_heads(g_far[:, c])], 0)
        q_all = jnp.concatenate([two_heads(q[:, c]), two_heads(q_far[:, c])], 0)
        dv[:, c] = dot(p_all, g_all, NN).astype(BF16)
        dk[:, c] = (dot(ds_all, q_all, NN) * SCALE).astype(BF16)
        for kind, (held, to) in enumerate(((out, out_hbm), (dk, dk_hbm), (dv, dv_hbm))):
            copy = pltpu.make_async_copy(held.at[:, c], to.at[:, c], sems.at[3 * p + kind])
            copy.start()
            copies.append(copy)
    for copy in copies:
        copy.wait()


def passed_along(block, distance):
    count = lax.axis_size("seq")
    route = [((i - distance) % count, i) for i in range(count)]
    return lax.ppermute(block, "seq", route)


def call(body, name, ins, outs, scratch=()):
    return pl.pallas_call(
        body,
        in_specs=[place for x, place in ins],
        out_specs=[place for shape, kind, place in outs],
        out_shape=[jax.ShapeDtypeStruct(shape, kind) for shape, kind, place in outs],
        scratch_shapes=scratch,
        compiler_params=pltpu.CompilerParams(vmem_limit_bytes=20 << 20),
        cost_estimate=pl.CostEstimate(
            flops=1 << 30, bytes_accessed=4 << 20, transcendentals=0
        ),
        name=name,
    )(*[x for x, place in ins])


def per_device(queries, keys, values, cotangent, neighbour_ids, neighbour_counts):
    dma = pltpu.SemaphoreType.DMA
    pool, tokens, pairs = (ROWS, WIDTH), (GROUP, WIDTH), (ROWS, WIDTH // 2)
    longer = (GROUP, WIDTH + HD)
    q_far = passed_along(queries, 1)
    ids = jnp.transpose(neighbour_ids)
    stats, numer, w_own, dp_own, bias_far, q, g, k, v = call(
        own_forward,
        "own_forward",
        [
            (pltpu.with_memory_space_constraint(x, pltpu.HBM), HBM)
            for x in (ids, neighbour_counts, queries, cotangent, keys, values)
        ],
        [
            ((24, HD), F32, VMEM), (tokens, F32, VMEM), (pairs, BF16, VMEM), (pairs, BF16, VMEM),
            ((8, HD), F32, VMEM), (tokens, BF16, VMEM), (longer, BF16, VMEM), (pool, BF16, VMEM),
            (pool, BF16, VMEM),
        ],
        [
            pltpu.SMEM(ids.shape, jnp.int32),
            pltpu.SMEM(neighbour_counts.shape, jnp.int32),
            dma((2 + 2 * len(LOADS),)),
        ],
    )
    g_far = passed_along(g, 1)
    message, w_far, stats_far = call(
        far_forward,
        "far_forward",
        [(x, VMEM) for x in (bias_far, q_far, k, v)],
        [(longer, BF16, VMEM), (pairs, BF16, VMEM), ((16, HD), F32, VMEM)],
    )
    message_back = passed_along(message, -1)
    dq_far, p_far, ds_far = call(
        far_backward,
        "far_backward",
        [(x, VMEM) for x in (g_far, k, v, w_far, message, stats_far)],
        [(tokens, BF16, VMEM), (pairs, BF16, VMEM), (pairs, BF16, VMEM)],
    )
    dq_back = passed_along(dq_far, -1)
    out, dq_own, dk, dv = call(
        finish,
        "finish",
        [
            (x, VMEM)
            for x in (
                q, g, q_far, g_far, k, w_own, dp_own, p_far, ds_far, numer, message_back, stats
            )
        ],
        [(tokens, BF16, HBM), (tokens, F32, VMEM), (pool, BF16, HBM), (pool, BF16, HBM)],
        [
            pltpu.VMEM(tokens, BF16), pltpu.VMEM(pool, BF16), pltpu.VMEM(pool, BF16),
            dma((3 * PAIRS,)),
        ],
    )
    query_grad = (dq_own + dq_back.astype(F32)).astype(BF16)
    return (out, query_grad, dk, dv)


def solution(mesh):
    split = P(("pop", "seq"), None)
    return jax.shard_map(
        per_device,
        mesh=mesh,
        in_specs=(split, split, split, split, P("pop", None), P("pop")),
        out_specs=(split, split, split, split),
        check_vma=False,
    )
```

```python
import math

import jax
import jax.numpy as jnp
from jax import lax
from jax.experimental import pallas as pl
from jax.experimental.pallas import tpu as pltpu
from jax.sharding import PartitionSpec as P

HD = 128
GROUP = 64
NLEN = 128
SLOTS = 8
HELD = 4
WIDTH = 2048
PAIR = 2 * HD
PAIRS = WIDTH // PAIR
ROWS = HELD * NLEN
SCALE = 1.0 / math.sqrt(HD)
TO_LOG2 = SCALE / math.log(2.0)
DEAD = -1e30
LOADS = (0, 2, 5, 8)
BF16 = jnp.bfloat16
F32 = jnp.float32
NT = (((1,), (1,)), ((), ()))
NN = (((1,), (0,)), ((), ()))
TN = (((0,), (0,)), ((), ()))
VMEM = pl.BlockSpec(memory_space=pltpu.VMEM)
HBM = pl.BlockSpec(memory_space=pltpu.HBM)


def dot(a, b, dims):
    return lax.dot_general(a, b, dims, preferred_element_type=F32)


def wide(p):
    return slice(p * PAIR, (p + 1) * PAIR)


def half(p):
    return slice(p * HD, (p + 1) * HD)


def two_heads(x):
    zero = jnp.zeros((GROUP, HD), x.dtype)
    first = jnp.concatenate([x[:, :HD], zero], 1)
    second = jnp.concatenate([zero, x[:, HD:]], 1)
    return jnp.concatenate([first, second], 0)


def own_columns(x):
    return jnp.concatenate([x[:GROUP, :HD], x[GROUP:, HD:]], 1)


def head_sums(x):
    tall = jnp.concatenate([x[:, :HD], x[:, HD:]], 0)
    return jnp.sum(jnp.transpose(tall), axis=0, keepdims=True)


def as_columns(rows):
    return jnp.transpose(jnp.concatenate([rows, jnp.zeros((HD - PAIRS, HD), F32)], 0))


def spread(columns, p):
    tall = jnp.broadcast_to(columns[:, p : p + 1], (2 * GROUP, HD))
    return jnp.concatenate([tall[:GROUP], tall[GROUP:]], 1)


def live_bias(ids, counts, group, first, n):
    hit = jnp.int32(0)
    for j in range(SLOTS):
        match = (ids[j, group] == first + n) & (j < counts[group])
        hit = hit | match.astype(jnp.int32)
    return jnp.where(hit > 0, F32(0.0), F32(DEAD))


def score_blocks(a, b):
    return [dot(a[n * NLEN : (n + 1) * NLEN], b, NT) for n in range(HELD)]


def softmax_part(raw, bias):
    peaks = [
        jnp.max(raw[n], axis=0, keepdims=True) * TO_LOG2 + bias[n] for n in range(HELD)
    ]
    peak = jnp.maximum(jnp.maximum(peaks[0], peaks[1]), jnp.maximum(peaks[2], peaks[3]))
    e = [
        jnp.exp2(raw[n] * TO_LOG2 - jnp.where(bias[n] < 0.0, F32(-DEAD), peak))
        for n in range(HELD)
    ]
    sums = [jnp.sum(x, axis=0, keepdims=True) for x in e]
    return ([x.astype(BF16) for x in e], peak, (sums[0] + sums[1]) + (sums[2] + sums[3]))


def staggered(stages):
    held = {}
    for t in range(PAIRS + len(stages) - 1):
        for lag, stage in enumerate(stages):
            p = t - lag
            if 0 <= p < PAIRS:
                held[p] = stage(p, held.get(p))


def merged(peak_a, total_a, peak_b, total_b):
    top = jnp.maximum(peak_a, peak_b)
    a = jnp.exp2(peak_a - top)
    b = jnp.exp2(peak_b - top)
    inv = 1.0 / (a * total_a + b * total_b)
    return (a * inv, b * inv)


def pieces(x, count):
    out = []
    for _ in range(count - 1):
        out.append(x.astype(BF16).astype(F32))
        x = x - out[-1]
    return out + [x]


def packed(figures):
    tall = []
    for rows, count in figures:
        tall += pieces(jnp.concatenate([rows[:, :GROUP], rows[:, GROUP:]], 0), count)
    tall = jnp.concatenate(tall + [jnp.zeros((HD - 16 * len(tall), GROUP), F32)], 0)
    tall = jnp.concatenate([tall, jnp.zeros((HD, GROUP), F32)], 1)
    return jnp.transpose(tall)[:GROUP].astype(BF16)


def unpacked(block, counts):
    tall = jnp.transpose(jnp.concatenate([block.astype(F32), jnp.zeros((GROUP, HD), F32)], 0))
    out, at = [], 0
    for count in counts:
        x = tall[at : at + 16]
        for n in range(1, count):
            x = x + tall[at + 16 * n : at + 16 * n + 16]
        out.append(jnp.concatenate([x[:PAIRS, :GROUP], x[PAIRS:, :GROUP]], 1))
        at += 16 * count
    return out


def rows_of(n):
    return slice(n * NLEN, (n + 1) * NLEN)


def own_forward(
    ids_hbm, counts_hbm, q_hbm, g_hbm, k_hbm, v_hbm,
    stats, numer, weights, q, g, k, v,
    ids, counts, sems,
):
    copies = [
        pltpu.make_async_copy(ids_hbm, ids, sems.at[0]),
        pltpu.make_async_copy(counts_hbm, counts, sems.at[1]),
        pltpu.make_async_copy(q_hbm, q, sems.at[2]),
        pltpu.make_async_copy(g_hbm, g.at[:, :WIDTH], sems.at[3]),
    ]
    for n in range(len(LOADS) - 1):
        c = slice(LOADS[n] * PAIR, LOADS[n + 1] * PAIR)
        copies.append(pltpu.make_async_copy(k_hbm.at[:, c], k.at[:, c], sems.at[4 + 2 * n]))
        copies.append(pltpu.make_async_copy(v_hbm.at[:, c], v.at[:, c], sems.at[5 + 2 * n]))
    for copy in copies:
        copy.start()
    index = lax.axis_index("seq")
    copies[0].wait()
    copies[1].wait()
    bias = [live_bias(ids, counts, index, index * HELD, n) for n in range(HELD)]
    copies[2].wait()
    copies[3].wait()

    def scores(p, _):
        if p in LOADS:
            n = LOADS.index(p)
            copies[4 + 2 * n].wait()
            copies[5 + 2 * n].wait()
        return score_blocks(k[:, wide(p)], two_heads(q[:, wide(p)]))

    def softmax(p, raw):
        e, peak, total = softmax_part(raw, bias)
        for n in range(HELD):
            weights[rows_of(n), half(p)] = e[n]
        stats[p : p + 1, :] = peak
        stats[8 + p : 9 + p, :] = total
        return e

    def sums(p, e):
        c = wide(p)
        part = own_columns(dot(jnp.concatenate(e, 0), v[:, c], TN))
        numer[:, c] = part
        return part

    def dots(p, part):
        stats[16 + p : 17 + p, :] = head_sums(part * g[:, wide(p)].astype(F32))

    staggered([scores, softmax, sums, dots])
    g[:, WIDTH:] = packed([(stats[:8, :], 3), (stats[8:16, :], 2), (stats[16:, :], 2)])


def own_dprob(ids_hbm, counts_hbm, g, v, dprob, bias_far, ids, counts, sems):
    copies = [
        pltpu.make_async_copy(ids_hbm, ids, sems.at[0]),
        pltpu.make_async_copy(counts_hbm, counts, sems.at[1]),
    ]
    for copy in copies:
        copy.start()
    for p in range(PAIRS):
        c, h = wide(p), half(p)
        blocks = score_blocks(v[:, c], two_heads(g[:, c]))
        for n in range(HELD):
            dprob[rows_of(n), h] = blocks[n].astype(BF16)
    for copy in copies:
        copy.wait()
    index = lax.axis_index("seq")
    before = lax.rem(index + lax.axis_size("seq") - 1, lax.axis_size("seq"))
    for n in range(HELD):
        bias_far[n : n + 1, :] = jnp.full(
            (1, HD), live_bias(ids, counts, before, index * HELD, n), F32
        )
    bias_far[HELD:, :] = jnp.zeros((8 - HELD, HD), F32)


def far_forward(bias_ref, q, k, v, message, weights, stats):
    bias = [bias_ref[n : n + 1, :] for n in range(HELD)]

    def scores(p, _):
        return score_blocks(k[:, wide(p)], two_heads(q[:, wide(p)]))

    def softmax(p, raw):
        e, peak, total = softmax_part(raw, bias)
        for n in range(HELD):
            weights[rows_of(n), half(p)] = e[n]
        stats[p : p + 1, :] = peak
        stats[8 + p : 9 + p, :] = total
        return e

    def sums(p, e):
        part = dot(jnp.concatenate(e, 0), v[:, wide(p)], TN)
        message[:, wide(p)] = own_columns(part).astype(BF16)

    staggered([scores, softmax, sums])
    message[:, WIDTH:] = packed([(stats[:8, :], 3), (stats[8:, :], 2)])


def far_backward(g, k, v, weights, message, stats, dq, prob, dscore):
    peak_own, total_own, dot_own = unpacked(g[:, WIDTH:], (3, 2, 2))
    own, far = merged(peak_own, total_own, stats[0:8, :], stats[8:16, :])
    delta_own = own * dot_own

    def dprobs(p, _):
        gg = g[:, wide(p)]
        dots = head_sums(message[:, wide(p)].astype(F32) * gg.astype(F32))
        delta = delta_own[p : p + 1] + far[p : p + 1] * dots
        return (score_blocks(v[:, wide(p)], two_heads(gg)), delta)

    def dscores(p, held):
        dp, delta = held
        out = []
        for n in range(HELD):
            r, h = rows_of(n), half(p)
            pr = weights[r, h].astype(F32) * far[p : p + 1]
            out.append((pr * (dp[n] - delta)).astype(BF16))
            prob[r, h] = pr.astype(BF16)
            dscore[r, h] = out[n]
        return out

    def dqueries(p, ds):
        part = own_columns(dot(jnp.concatenate(ds, 0), k[:, wide(p)], TN))
        dq[:, wide(p)] = (part * SCALE).astype(BF16)

    staggered([dprobs, dscores, dqueries])


def finish(
    q, g, q_far, g_far, k, w_own, dp_own, p_far, ds_far, numer, message, stats,
    out_hbm, dq, dk_hbm, dv_hbm,
    out, dk, dv, sems,
):
    peak_far, total_far = unpacked(message[:, WIDTH:], (3, 2))
    own, far = merged(stats[0:8, :], stats[8:16, :], peak_far, total_far)
    own_tall, far_tall = as_columns(own), as_columns(far)
    copies = []
    for p in range(PAIRS):
        c, h = wide(p), half(p)
        row = slice(p, p + 1)
        gg = g[:, c]
        attended = (
            numer[:, c] * spread(own_tall, p) + message[:, c].astype(F32) * spread(far_tall, p)
        ).astype(BF16)
        out[:, c] = attended
        delta = head_sums(gg.astype(F32) * attended.astype(F32))
        pr = w_own[:, h].astype(F32) * own[row]
        ds = (pr * (dp_own[:, h].astype(F32) - delta)).astype(BF16)
        dq[:, c] = own_columns(dot(ds, k[:, c], TN)) * SCALE
        p_all = jnp.concatenate([pr.astype(BF16), p_far[:, h]], 1)
        ds_all = jnp.concatenate([ds, ds_far[:, h]], 1)
        g_all = jnp.concatenate([two_heads(gg), two_heads(g_far[:, c])], 0)
        q_all = jnp.concatenate([two_heads(q[:, c]), two_heads(q_far[:, c])], 0)
        dv[:, c] = dot(p_all, g_all, NN).astype(BF16)
        dk[:, c] = (dot(ds_all, q_all, NN) * SCALE).astype(BF16)
        for kind, (held, to) in enumerate(((out, out_hbm), (dk, dk_hbm), (dv, dv_hbm))):
            copy = pltpu.make_async_copy(held.at[:, c], to.at[:, c], sems.at[3 * p + kind])
            copy.start()
            copies.append(copy)
    for copy in copies:
        copy.wait()


def passed_along(block, distance):
    count = lax.axis_size("seq")
    route = [((i - distance) % count, i) for i in range(count)]
    return lax.ppermute(block, "seq", route)


def call(body, name, ins, outs, scratch=()):
    return pl.pallas_call(
        body,
        in_specs=[place for x, place in ins],
        out_specs=[place for shape, kind, place in outs],
        out_shape=[jax.ShapeDtypeStruct(shape, kind) for shape, kind, place in outs],
        scratch_shapes=scratch,
        compiler_params=pltpu.CompilerParams(vmem_limit_bytes=20 << 20),
        cost_estimate=pl.CostEstimate(
            flops=1 << 30, bytes_accessed=4 << 20, transcendentals=0
        ),
        name=name,
    )(*[x for x, place in ins])


def per_device(queries, keys, values, cotangent, neighbour_ids, neighbour_counts):
    dma = pltpu.SemaphoreType.DMA
    pool, tokens, pairs = (ROWS, WIDTH), (GROUP, WIDTH), (ROWS, WIDTH // 2)
    longer = (GROUP, WIDTH + HD)
    q_far = passed_along(queries, 1)
    ids = jnp.transpose(neighbour_ids)
    in_hbm = [
        (pltpu.with_memory_space_constraint(x, pltpu.HBM), HBM)
        for x in (ids, neighbour_counts, queries, cotangent, keys, values)
    ]
    tables = [pltpu.SMEM(ids.shape, jnp.int32), pltpu.SMEM(neighbour_counts.shape, jnp.int32)]
    stats, numer, w_own, q, g, k, v = call(
        own_forward,
        "own_forward",
        in_hbm,
        [
            ((24, HD), F32, VMEM), (tokens, F32, VMEM), (pairs, BF16, VMEM),
            (tokens, BF16, VMEM), (longer, BF16, VMEM), (pool, BF16, VMEM), (pool, BF16, VMEM),
        ],
        tables + [dma((2 + 2 * len(LOADS),))],
    )
    g_far = passed_along(g, 1)
    dp_own, bias_far = call(
        own_dprob,
        "own_dprob",
        in_hbm[:2] + [(g, VMEM), (v, VMEM)],
        [(pairs, BF16, VMEM), ((8, HD), F32, VMEM)],
        tables + [dma((2,))],
    )
    message, w_far, stats_far = call(
        far_forward,
        "far_forward",
        [(x, VMEM) for x in (bias_far, q_far, k, v)],
        [(longer, BF16, VMEM), (pairs, BF16, VMEM), ((16, HD), F32, VMEM)],
    )
    message_back = passed_along(message, -1)
    dq_far, p_far, ds_far = call(
        far_backward,
        "far_backward",
        [(x, VMEM) for x in (g_far, k, v, w_far, message, stats_far)],
        [(tokens, BF16, VMEM), (pairs, BF16, VMEM), (pairs, BF16, VMEM)],
    )
    dq_back = passed_along(dq_far, -1)
    out, dq_own, dk, dv = call(
        finish,
        "finish",
        [
            (x, VMEM)
            for x in (
                q, g, q_far, g_far, k, w_own, dp_own, p_far, ds_far, numer, message_back, stats
            )
        ],
        [(tokens, BF16, HBM), (tokens, F32, VMEM), (pool, BF16, HBM), (pool, BF16, HBM)],
        [
            pltpu.VMEM(tokens, BF16), pltpu.VMEM(pool, BF16), pltpu.VMEM(pool, BF16),
            dma((3 * PAIRS,)),
        ],
    )
    query_grad = (dq_own + dq_back.astype(F32)).astype(BF16)
    return (out, query_grad, dk, dv)


def solution(mesh):
    split = P(("pop", "seq"), None)
    return jax.shard_map(
        per_device,
        mesh=mesh,
        in_specs=(split, split, split, split, P("pop", None), P("pop")),
        out_specs=(split, split, split, split),
        check_vma=False,
    )
```

```python
import math

import jax
import jax.numpy as jnp
from jax import lax
from jax.experimental import pallas as pl
from jax.experimental.pallas import tpu as pltpu
from jax.sharding import PartitionSpec as P

HD = 128
GROUP = 64
NLEN = 128
SLOTS = 8
HELD = 4
WIDTH = 2048
PAIR = 2 * HD
PAIRS = WIDTH // PAIR
ROWS = HELD * NLEN
SCALE = 1.0 / math.sqrt(HD)
TO_LOG2 = SCALE / math.log(2.0)
DEAD = -1e30
LOADS = (0, 2, 5, 8)
SENT = PAIRS - 1
BF16 = jnp.bfloat16
F32 = jnp.float32
NT = (((1,), (1,)), ((), ()))
NN = (((1,), (0,)), ((), ()))
TN = (((0,), (0,)), ((), ()))
VMEM = pl.BlockSpec(memory_space=pltpu.VMEM)
HBM = pl.BlockSpec(memory_space=pltpu.HBM)


def dot(a, b, dims):
    return lax.dot_general(a, b, dims, preferred_element_type=F32)


def wide(p):
    return slice(p * PAIR, (p + 1) * PAIR)


def half(p):
    return slice(p * HD, (p + 1) * HD)


def two_heads(x):
    zero = jnp.zeros((GROUP, HD), x.dtype)
    first = jnp.concatenate([x[:, :HD], zero], 1)
    second = jnp.concatenate([zero, x[:, HD:]], 1)
    return jnp.concatenate([first, second], 0)


def own_columns(x):
    return jnp.concatenate([x[:GROUP, :HD], x[GROUP:, HD:]], 1)


def head_sums(x):
    tall = jnp.concatenate([x[:, :HD], x[:, HD:]], 0)
    high = tall.astype(BF16)
    low = (tall - high.astype(F32)).astype(BF16)
    return dot(jnp.ones((16, PAIR), BF16), jnp.concatenate([high, low], 1), NT)[0:1]


def as_columns(rows):
    return jnp.transpose(jnp.concatenate([rows, jnp.zeros((HD - PAIRS, HD), F32)], 0))


def spread(columns, p):
    tall = jnp.broadcast_to(columns[:, p : p + 1], (2 * GROUP, HD))
    return jnp.concatenate([tall[:GROUP], tall[GROUP:]], 1)


def live_bias(ids, counts, group, first, n):
    hit = jnp.int32(0)
    for j in range(SLOTS):
        match = (ids[j, group] == first + n) & (j < counts[group])
        hit = hit | match.astype(jnp.int32)
    return jnp.where(hit > 0, F32(0.0), F32(DEAD))


def score_blocks(a, b):
    return [dot(a[n * NLEN : (n + 1) * NLEN], b, NT) for n in range(HELD)]


def softmax_part(raw, bias):
    peaks = [
        jnp.max(raw[n], axis=0, keepdims=True) * TO_LOG2 + bias[n] for n in range(HELD)
    ]
    peak = jnp.maximum(jnp.maximum(peaks[0], peaks[1]), jnp.maximum(peaks[2], peaks[3]))
    e = [
        jnp.exp2(raw[n] * TO_LOG2 - jnp.where(bias[n] < 0.0, F32(-DEAD), peak))
        for n in range(HELD)
    ]
    sums = [jnp.sum(x, axis=0, keepdims=True) for x in e]
    return ([x.astype(BF16) for x in e], peak, (sums[0] + sums[1]) + (sums[2] + sums[3]))


def staggered(stages):
    held = {}
    for t in range(PAIRS + len(stages) - 1):
        for lag, stage in enumerate(stages):
            p = t - lag
            if 0 <= p < PAIRS:
                held[p] = stage(p, held.get(p))


def merged(peak_a, total_a, peak_b, total_b):
    top = jnp.maximum(peak_a, peak_b)
    a = jnp.exp2(peak_a - top)
    b = jnp.exp2(peak_b - top)
    inv = 1.0 / (a * total_a + b * total_b)
    return (a * inv, b * inv)


def pieces(x, count):
    out = []
    for _ in range(count - 1):
        out.append(x.astype(BF16).astype(F32))
        x = x - out[-1]
    return out + [x]


def packed(figures):
    tall = []
    for rows, count in figures:
        tall += pieces(jnp.concatenate([rows[:, :GROUP], rows[:, GROUP:]], 0), count)
    tall = jnp.concatenate(tall + [jnp.zeros((HD - 16 * len(tall), GROUP), F32)], 0)
    tall = jnp.concatenate([tall, jnp.zeros((HD, GROUP), F32)], 1)
    return jnp.transpose(tall)[:GROUP].astype(BF16)


def unpacked(block, counts):
    tall = jnp.transpose(jnp.concatenate([block.astype(F32), jnp.zeros((GROUP, HD), F32)], 0))
    out, at = [], 0
    for count in counts:
        x = tall[at : at + 16]
        for n in range(1, count):
            x = x + tall[at + 16 * n : at + 16 * n + 16]
        out.append(jnp.concatenate([x[:PAIRS, :GROUP], x[PAIRS:, :GROUP]], 1))
        at += 16 * count
    return out


def rows_of(n):
    return slice(n * NLEN, (n + 1) * NLEN)


def own_forward(
    ids_hbm, counts_hbm, q_hbm, g_hbm, k_hbm, v_hbm,
    stats, numer, weights, q, g, k, v,
    ids, counts, sems,
):
    copies = [
        pltpu.make_async_copy(ids_hbm, ids, sems.at[0]),
        pltpu.make_async_copy(counts_hbm, counts, sems.at[1]),
        pltpu.make_async_copy(q_hbm, q, sems.at[2]),
        pltpu.make_async_copy(g_hbm, g.at[:, :WIDTH], sems.at[3]),
    ]
    for n in range(len(LOADS) - 1):
        c = slice(LOADS[n] * PAIR, LOADS[n + 1] * PAIR)
        copies.append(pltpu.make_async_copy(k_hbm.at[:, c], k.at[:, c], sems.at[4 + 2 * n]))
        copies.append(pltpu.make_async_copy(v_hbm.at[:, c], v.at[:, c], sems.at[5 + 2 * n]))
    for copy in copies:
        copy.start()
    index = lax.axis_index("seq")
    copies[0].wait()
    copies[1].wait()
    bias = [live_bias(ids, counts, index, index * HELD, n) for n in range(HELD)]
    copies[2].wait()
    copies[3].wait()

    def scores(p, _):
        if p in LOADS:
            n = LOADS.index(p)
            copies[4 + 2 * n].wait()
            copies[5 + 2 * n].wait()
        return score_blocks(k[:, wide(p)], two_heads(q[:, wide(p)]))

    def softmax(p, raw):
        e, peak, total = softmax_part(raw, bias)
        for n in range(HELD):
            weights[rows_of(n), half(p)] = e[n]
        stats[p : p + 1, :] = peak
        stats[8 + p : 9 + p, :] = total
        return e

    def sums(p, e):
        c = wide(p)
        part = own_columns(dot(jnp.concatenate(e, 0), v[:, c], TN))
        numer[:, c] = part
        return part

    def dots(p, part):
        stats[16 + p : 17 + p, :] = head_sums(part * g[:, wide(p)].astype(F32))

    staggered([scores, softmax, sums, dots])
    g[:, WIDTH:] = packed([(stats[:8, :], 3), (stats[8:16, :], 2), (stats[16:, :], 2)])


def own_dprob(ids_hbm, counts_hbm, g, v, dprob, bias_far, ids, counts, sems):
    copies = [
        pltpu.make_async_copy(ids_hbm, ids, sems.at[0]),
        pltpu.make_async_copy(counts_hbm, counts, sems.at[1]),
    ]
    for copy in copies:
        copy.start()
    for p in range(PAIRS):
        c, h = wide(p), half(p)
        blocks = score_blocks(v[:, c], two_heads(g[:, c]))
        for n in range(HELD):
            dprob[rows_of(n), h] = blocks[n].astype(BF16)
    for copy in copies:
        copy.wait()
    index = lax.axis_index("seq")
    before = lax.rem(index + lax.axis_size("seq") - 1, lax.axis_size("seq"))
    for n in range(HELD):
        bias_far[n : n + 1, :] = jnp.full(
            (1, HD), live_bias(ids, counts, before, index * HELD, n), F32
        )
    bias_far[HELD:, :] = jnp.zeros((8 - HELD, HD), F32)


def far_forward(bias_ref, q, k, v, message, weights, stats):
    bias = [bias_ref[n : n + 1, :] for n in range(HELD)]

    def scores(p, _):
        return score_blocks(k[:, wide(p)], two_heads(q[:, wide(p)]))

    def softmax(p, raw):
        e, peak, total = softmax_part(raw, bias)
        for n in range(HELD):
            weights[rows_of(n), half(p)] = e[n]
        stats[p : p + 1, :] = peak
        stats[8 + p : 9 + p, :] = total
        return e

    def sums(p, e):
        part = dot(jnp.concatenate(e, 0), v[:, wide(p)], TN)
        message[:, wide(p)] = own_columns(part).astype(BF16)

    staggered([scores, softmax, sums])
    message[:, WIDTH:] = packed([(stats[:8, :], 3), (stats[8:, :], 2)])


def far_backward(g, k, v, weights, message, stats, dq, prob, dscore):
    peak_own, total_own, dot_own = unpacked(g[:, WIDTH:], (3, 2, 2))
    own, far = merged(peak_own, total_own, stats[0:8, :], stats[8:16, :])
    delta_own = own * dot_own

    def dprobs(p, _):
        gg = g[:, wide(p)]
        dots = head_sums(message[:, wide(p)].astype(F32) * gg.astype(F32))
        delta = delta_own[p : p + 1] + far[p : p + 1] * dots
        return (score_blocks(v[:, wide(p)], two_heads(gg)), delta)

    def dscores(p, held):
        dp, delta = held
        out = []
        for n in range(HELD):
            r, h = rows_of(n), half(p)
            pr = weights[r, h].astype(F32) * far[p : p + 1]
            out.append((pr * (dp[n] - delta)).astype(BF16))
            prob[r, h] = pr.astype(BF16)
            dscore[r, h] = out[n]
        return out

    def dqueries(p, ds):
        part = own_columns(dot(jnp.concatenate(ds, 0), k[:, wide(p)], TN))
        dq[:, wide(p)] = (part * SCALE).astype(BF16)

    staggered([dprobs, dscores, dqueries])


def gradients(
    q, g, q_far, g_far, k, w_own, dp_own, p_far, ds_far, numer, message, stats,
    out_hbm, dq, dk_hbm, dv_hbm, dk_last, dv_last,
    out, dk, dv, sems,
):
    peak_far, total_far = unpacked(message[:, WIDTH:], (3, 2))
    own, far = merged(stats[0:8, :], stats[8:16, :], peak_far, total_far)
    own_tall, far_tall = as_columns(own), as_columns(far)
    copies = []

    def send(x, to):
        copies.append(pltpu.make_async_copy(x, to, sems.at[len(copies)]))
        copies[-1].start()

    def merge(p, _):
        c = wide(p)
        attended = (
            numer[:, c] * spread(own_tall, p) + message[:, c].astype(F32) * spread(far_tall, p)
        ).astype(BF16)
        out[:, c] = attended
        if p == PAIRS - 1:
            send(out, out_hbm)
        return head_sums(g[:, c].astype(F32) * attended.astype(F32))

    def dscores(p, delta):
        h = half(p)
        pr = w_own[:, h].astype(F32) * own[p : p + 1]
        ds = (pr * (dp_own[:, h].astype(F32) - delta)).astype(BF16)
        return (pr.astype(BF16), ds)

    def sums(p, held):
        pr, ds = held
        c, h = wide(p), half(p)
        dq[:, c] = own_columns(dot(ds, k[:, c], TN)) * SCALE
        p_all = jnp.concatenate([pr, p_far[:, h]], 1)
        ds_all = jnp.concatenate([ds, ds_far[:, h]], 1)
        g_all = jnp.concatenate([two_heads(g[:, c]), two_heads(g_far[:, c])], 0)
        q_all = jnp.concatenate([two_heads(q[:, c]), two_heads(q_far[:, c])], 0)
        dv_pair = dot(p_all, g_all, NN).astype(BF16)
        dk_pair = (dot(ds_all, q_all, NN) * SCALE).astype(BF16)
        if p < SENT:
            dv[:, c] = dv_pair
            dk[:, c] = dk_pair
            send(dv.at[:, c], dv_hbm.at[:, c])
            send(dk.at[:, c], dk_hbm.at[:, c])
        else:
            dv_last[:, wide(p - SENT)] = dv_pair
            dk_last[:, wide(p - SENT)] = dk_pair

    staggered([merge, dscores, sums])
    for copy in copies:
        copy.wait()


def last_copies(
    dk_in, dv_in, dk_last, dv_last, dq_own, dq_far, dk_hbm, dv_hbm, dq_hbm, dq, sems
):
    rest = slice(SENT * PAIR, WIDTH)
    copies = [
        pltpu.make_async_copy(dk_last, dk_hbm.at[:, rest], sems.at[0]),
        pltpu.make_async_copy(dv_last, dv_hbm.at[:, rest], sems.at[1]),
        pltpu.make_async_copy(dq, dq_hbm, sems.at[2]),
    ]
    copies[0].start()
    copies[1].start()
    dq[...] = (dq_own[...] + dq_far[...].astype(F32)).astype(BF16)
    copies[2].start()
    for copy in copies:
        copy.wait()


def passed_along(block, distance):
    count = lax.axis_size("seq")
    route = [((i - distance) % count, i) for i in range(count)]
    return lax.ppermute(block, "seq", route)


def call(body, name, ins, outs, scratch=(), aliases=None):
    return pl.pallas_call(
        body,
        in_specs=[place for x, place in ins],
        out_specs=[place for shape, kind, place in outs],
        out_shape=[jax.ShapeDtypeStruct(shape, kind) for shape, kind, place in outs],
        scratch_shapes=scratch,
        input_output_aliases=aliases or {},
        compiler_params=pltpu.CompilerParams(vmem_limit_bytes=20 << 20),
        cost_estimate=pl.CostEstimate(
            flops=1 << 30, bytes_accessed=4 << 20, transcendentals=0
        ),
        name=name,
    )(*[x for x, place in ins])


def per_device(queries, keys, values, cotangent, neighbour_ids, neighbour_counts):
    dma = pltpu.SemaphoreType.DMA
    pool, tokens, pairs = (ROWS, WIDTH), (GROUP, WIDTH), (ROWS, WIDTH // 2)
    longer = (GROUP, WIDTH + HD)
    q_far = passed_along(queries, 1)
    ids = jnp.transpose(neighbour_ids)
    in_hbm = [
        (pltpu.with_memory_space_constraint(x, pltpu.HBM), HBM)
        for x in (ids, neighbour_counts, queries, cotangent, keys, values)
    ]
    tables = [pltpu.SMEM(ids.shape, jnp.int32), pltpu.SMEM(neighbour_counts.shape, jnp.int32)]
    stats, numer, w_own, q, g, k, v = call(
        own_forward,
        "own_forward",
        in_hbm,
        [
            ((24, HD), F32, VMEM), (tokens, F32, VMEM), (pairs, BF16, VMEM),
            (tokens, BF16, VMEM), (longer, BF16, VMEM), (pool, BF16, VMEM), (pool, BF16, VMEM),
        ],
        tables + [dma((2 + 2 * len(LOADS),))],
    )
    g_far = passed_along(g, 1)
    dp_own, bias_far = call(
        own_dprob,
        "own_dprob",
        in_hbm[:2] + [(g, VMEM), (v, VMEM)],
        [(pairs, BF16, VMEM), ((8, HD), F32, VMEM)],
        tables + [dma((2,))],
    )
    message, w_far, stats_far = call(
        far_forward,
        "far_forward",
        [(x, VMEM) for x in (bias_far, q_far, k, v)],
        [(longer, BF16, VMEM), (pairs, BF16, VMEM), ((16, HD), F32, VMEM)],
    )
    message_back = passed_along(message, -1)
    dq_far, p_far, ds_far = call(
        far_backward,
        "far_backward",
        [(x, VMEM) for x in (g_far, k, v, w_far, message, stats_far)],
        [(tokens, BF16, VMEM), (pairs, BF16, VMEM), (pairs, BF16, VMEM)],
    )
    dq_back = passed_along(dq_far, -1)
    rest = (ROWS, WIDTH - SENT * PAIR)
    out, dq_own, dk, dv, dk_last, dv_last = call(
        gradients,
        "gradients",
        [
            (x, VMEM)
            for x in (
                q, g, q_far, g_far, k, w_own, dp_own, p_far, ds_far, numer, message_back, stats
            )
        ],
        [
            (tokens, BF16, HBM), (tokens, F32, VMEM), (pool, BF16, HBM), (pool, BF16, HBM),
            (rest, BF16, VMEM), (rest, BF16, VMEM),
        ],
        [
            pltpu.VMEM(tokens, BF16), pltpu.VMEM(pool, BF16), pltpu.VMEM(pool, BF16),
            dma((1 + 2 * SENT,)),
        ],
    )
    dk, dv, query_grad = call(
        last_copies,
        "last_copies",
        [(dk, HBM), (dv, HBM)] + [(x, VMEM) for x in (dk_last, dv_last, dq_own, dq_back)],
        [(pool, BF16, HBM), (pool, BF16, HBM), (tokens, BF16, HBM)],
        [pltpu.VMEM(tokens, BF16), dma((3,))],
        {0: 0, 1: 1},
    )
    return (out, query_grad, dk, dv)


def solution(mesh):
    split = P(("pop", "seq"), None)
    return jax.shard_map(
        per_device,
        mesh=mesh,
        in_specs=(split, split, split, split, P("pop", None), P("pop")),
        out_specs=(split, split, split, split),
        check_vma=False,
    )
```

```python
import math

import jax
import jax.numpy as jnp
from jax import lax
from jax.experimental import pallas as pl
from jax.experimental.pallas import tpu as pltpu
from jax.sharding import PartitionSpec as P

HD = 128
GROUP = 64
NLEN = 128
SLOTS = 8
HELD = 4
WIDTH = 2048
PAIR = 2 * HD
PAIRS = WIDTH // PAIR
ROWS = HELD * NLEN
SCALE = 1.0 / math.sqrt(HD)
TO_LOG2 = SCALE / math.log(2.0)
DEAD = -1e30
LOADS = (0, 2, 5, 8)
BF16 = jnp.bfloat16
F32 = jnp.float32
NT = (((1,), (1,)), ((), ()))
NN = (((1,), (0,)), ((), ()))
TN = (((0,), (0,)), ((), ()))
VMEM = pl.BlockSpec(memory_space=pltpu.VMEM)
HBM = pl.BlockSpec(memory_space=pltpu.HBM)


def dot(a, b, dims):
    return lax.dot_general(a, b, dims, preferred_element_type=F32)


def wide(p):
    return slice(p * PAIR, (p + 1) * PAIR)


def half(p):
    return slice(p * HD, (p + 1) * HD)


def two_heads(x):
    zero = jnp.zeros((GROUP, HD), x.dtype)
    first = jnp.concatenate([x[:, :HD], zero], 1)
    second = jnp.concatenate([zero, x[:, HD:]], 1)
    return jnp.concatenate([first, second], 0)


def own_columns(x):
    return jnp.concatenate([x[:GROUP, :HD], x[GROUP:, HD:]], 1)


def head_sums(x):
    tall = jnp.concatenate([x[:, :HD], x[:, HD:]], 0)
    high = tall.astype(BF16)
    low = (tall - high.astype(F32)).astype(BF16)
    return dot(jnp.ones((16, PAIR), BF16), jnp.concatenate([high, low], 1), NT)[0:1]


def head_sums_by_transpose(x):
    tall = jnp.concatenate([x[:, :HD], x[:, HD:]], 0)
    return jnp.sum(jnp.transpose(tall), axis=0, keepdims=True)


def as_columns(rows):
    empty = jnp.zeros((HD - PAIRS * len(rows), HD), F32)
    return jnp.transpose(jnp.concatenate(rows + [empty], 0))


def spread(columns, p):
    tall = jnp.broadcast_to(columns[:, p : p + 1], (2 * GROUP, HD))
    return jnp.concatenate([tall[:GROUP], tall[GROUP:]], 1)


def live_bias(ids, counts, group, first, n):
    hit = jnp.int32(0)
    for j in range(SLOTS):
        match = (ids[j, group] == first + n) & (j < counts[group])
        hit = hit | match.astype(jnp.int32)
    return jnp.where(hit > 0, F32(0.0), F32(DEAD))


def score_blocks(a, b):
    return [dot(a[n * NLEN : (n + 1) * NLEN], b, NT) for n in range(HELD)]


def softmax_part(raw, bias):
    peaks = [
        jnp.max(raw[n], axis=0, keepdims=True) * TO_LOG2 + bias[n] for n in range(HELD)
    ]
    peak = jnp.maximum(jnp.maximum(peaks[0], peaks[1]), jnp.maximum(peaks[2], peaks[3]))
    e = [
        jnp.exp2(raw[n] * TO_LOG2 - jnp.where(bias[n] < 0.0, F32(-DEAD), peak))
        for n in range(HELD)
    ]
    sums = [jnp.sum(x, axis=0, keepdims=True) for x in e]
    return ([x.astype(BF16) for x in e], peak, (sums[0] + sums[1]) + (sums[2] + sums[3]))


def staggered(stages):
    held = {}
    for t in range(PAIRS + len(stages) - 1):
        for lag, stage in enumerate(stages):
            p = t - lag
            if 0 <= p < PAIRS:
                held[p] = stage(p, held.get(p))


def merged(peak_a, total_a, peak_b, total_b):
    top = jnp.maximum(peak_a, peak_b)
    a = jnp.exp2(peak_a - top)
    b = jnp.exp2(peak_b - top)
    inv = 1.0 / (a * total_a + b * total_b)
    return (a * inv, b * inv)


def pieces(x, count):
    out = []
    for _ in range(count - 1):
        out.append(x.astype(BF16).astype(F32))
        x = x - out[-1]
    return out + [x]


def packed(figures):
    tall = []
    for rows, count in figures:
        tall += pieces(rows, count)
    tall += [jnp.zeros((PAIRS, HD), F32)] * (GROUP // PAIRS - len(tall))
    return jnp.concatenate(tall, 0).astype(BF16)


def unpacked(block, counts):
    tall = block.astype(F32)
    out, at = [], 0
    for count in counts:
        x = tall[at : at + PAIRS]
        for n in range(1, count):
            x = x + tall[at + PAIRS * n : at + PAIRS * (n + 1)]
        out.append(x)
        at += PAIRS * count
    return out


def rows_of(n):
    return slice(n * NLEN, (n + 1) * NLEN)


def own_forward(
    ids_hbm, counts_hbm, q_hbm, g_hbm, k_hbm, v_hbm,
    stats, numer, weights, q, g, k, v,
    ids, counts, sems,
):
    copies = [
        pltpu.make_async_copy(ids_hbm, ids, sems.at[0]),
        pltpu.make_async_copy(counts_hbm, counts, sems.at[1]),
        pltpu.make_async_copy(q_hbm, q, sems.at[2]),
        pltpu.make_async_copy(g_hbm, g.at[:, :WIDTH], sems.at[3]),
    ]
    for n in range(len(LOADS) - 1):
        c = slice(LOADS[n] * PAIR, LOADS[n + 1] * PAIR)
        copies.append(pltpu.make_async_copy(k_hbm.at[:, c], k.at[:, c], sems.at[4 + 2 * n]))
        copies.append(pltpu.make_async_copy(v_hbm.at[:, c], v.at[:, c], sems.at[5 + 2 * n]))
    for copy in copies:
        copy.start()
    index = lax.axis_index("seq")
    copies[0].wait()
    copies[1].wait()
    bias = [live_bias(ids, counts, index, index * HELD, n) for n in range(HELD)]
    copies[2].wait()
    copies[3].wait()

    def scores(p, _):
        if p in LOADS:
            n = LOADS.index(p)
            copies[4 + 2 * n].wait()
            copies[5 + 2 * n].wait()
        return score_blocks(k[:, wide(p)], two_heads(q[:, wide(p)]))

    def softmax(p, raw):
        e, peak, total = softmax_part(raw, bias)
        for n in range(HELD):
            weights[rows_of(n), half(p)] = e[n]
        stats[p : p + 1, :] = peak
        stats[8 + p : 9 + p, :] = total
        return e

    def sums(p, e):
        c = wide(p)
        part = own_columns(dot(jnp.concatenate(e, 0), v[:, c], TN))
        numer[:, c] = part
        return part

    def dots(p, part):
        stats[16 + p : 17 + p, :] = head_sums_by_transpose(part * g[:, wide(p)].astype(F32))

    staggered([scores, softmax, sums, dots])
    g[:, WIDTH:] = packed([(stats[:8, :], 3), (stats[8:16, :], 2), (stats[16:, :], 2)])


def own_dprob(ids_hbm, counts_hbm, g, v, dprob, bias_far, ids, counts, sems):
    copies = [
        pltpu.make_async_copy(ids_hbm, ids, sems.at[0]),
        pltpu.make_async_copy(counts_hbm, counts, sems.at[1]),
    ]
    for copy in copies:
        copy.start()
    for p in range(PAIRS):
        c, h = wide(p), half(p)
        blocks = score_blocks(v[:, c], two_heads(g[:, c]))
        for n in range(HELD):
            dprob[rows_of(n), h] = blocks[n].astype(BF16)
    for copy in copies:
        copy.wait()
    index = lax.axis_index("seq")
    before = lax.rem(index + lax.axis_size("seq") - 1, lax.axis_size("seq"))
    for n in range(HELD):
        bias_far[n : n + 1, :] = jnp.full(
            (1, HD), live_bias(ids, counts, before, index * HELD, n), F32
        )
    bias_far[HELD:, :] = jnp.zeros((8 - HELD, HD), F32)


def far_forward(bias_ref, q, k, v, message, weights, stats):
    bias = [bias_ref[n : n + 1, :] for n in range(HELD)]

    def scores(p, _):
        return score_blocks(k[:, wide(p)], two_heads(q[:, wide(p)]))

    def softmax(p, raw):
        e, peak, total = softmax_part(raw, bias)
        for n in range(HELD):
            weights[rows_of(n), half(p)] = e[n]
        stats[p : p + 1, :] = peak
        stats[8 + p : 9 + p, :] = total
        return e

    def sums(p, e):
        part = dot(jnp.concatenate(e, 0), v[:, wide(p)], TN)
        message[:, wide(p)] = own_columns(part).astype(BF16)

    staggered([scores, softmax, sums])
    message[:, WIDTH:] = packed([(stats[:8, :], 3), (stats[8:, :], 2)])


def far_backward(g, k, v, weights, message, stats, dq, prob, dscore):
    peak_own, total_own, dot_own = unpacked(g[:, WIDTH:], (3, 2, 2))
    own, far = merged(peak_own, total_own, stats[0:8, :], stats[8:16, :])
    delta_own = own * dot_own

    def dprobs(p, _):
        gg = g[:, wide(p)]
        dots = head_sums(message[:, wide(p)].astype(F32) * gg.astype(F32))
        delta = delta_own[p : p + 1] + far[p : p + 1] * dots
        return (score_blocks(v[:, wide(p)], two_heads(gg)), delta)

    def dscores(p, held):
        dp, delta = held
        out = []
        for n in range(HELD):
            r, h = rows_of(n), half(p)
            pr = weights[r, h].astype(F32) * far[p : p + 1]
            out.append((pr * (dp[n] - delta)).astype(BF16))
            prob[r, h] = pr.astype(BF16)
            dscore[r, h] = out[n]
        return out

    def dqueries(p, ds):
        part = own_columns(dot(jnp.concatenate(ds, 0), k[:, wide(p)], TN))
        dq[:, wide(p)] = (part * SCALE).astype(BF16)

    staggered([dprobs, dscores, dqueries])


def gradients(
    q, g, q_far, g_far, k, w_own, dp_own, p_far, ds_far, numer, message, stats,
    out_hbm, dq, dk_hbm, dv_hbm,
    out, dk, dv, sems,
):
    peak_far, total_far = unpacked(message[:, WIDTH:], (3, 2))
    own, far = merged(stats[0:8, :], stats[8:16, :], peak_far, total_far)
    factors = as_columns([own, far])
    copies = []

    def send(x, to):
        copies.append(pltpu.make_async_copy(x, to, sems.at[len(copies)]))
        copies[-1].start()

    def merge(p, _):
        c = wide(p)
        attended = (
            numer[:, c] * spread(factors, p)
            + message[:, c].astype(F32) * spread(factors, PAIRS + p)
        ).astype(BF16)
        out[:, c] = attended
        if p == PAIRS - 1:
            send(out, out_hbm)
        return head_sums(g[:, c].astype(F32) * attended.astype(F32))

    def dscores(p, delta):
        h = half(p)
        pr = w_own[:, h].astype(F32) * own[p : p + 1]
        ds = (pr * (dp_own[:, h].astype(F32) - delta)).astype(BF16)
        return (pr.astype(BF16), ds)

    def sums(p, held):
        pr, ds = held
        c, h = wide(p), half(p)
        dq[:, c] = own_columns(dot(ds, k[:, c], TN)) * SCALE
        p_all = jnp.concatenate([pr, p_far[:, h]], 1)
        ds_all = jnp.concatenate([ds, ds_far[:, h]], 1)
        g_all = jnp.concatenate([two_heads(g[:, c]), two_heads(g_far[:, c])], 0)
        q_all = jnp.concatenate([two_heads(q[:, c]), two_heads(q_far[:, c])], 0)
        dv_pair = dot(p_all, g_all, NN).astype(BF16)
        dk_pair = (dot(ds_all, q_all, NN) * SCALE).astype(BF16)
        dv[:, c] = dv_pair
        dk[:, c] = dk_pair
        send(dv.at[:, c], dv_hbm.at[:, c])
        send(dk.at[:, c], dk_hbm.at[:, c])

    staggered([merge, dscores, sums])
    for copy in copies:
        copy.wait()


def add_queries(own, far, total_hbm, total, sems):
    copies = []
    for n in range(2):
        c = slice(n * WIDTH // 2, (n + 1) * WIDTH // 2)
        total[:, c] = (own[:, c] + far[:, c].astype(F32)).astype(BF16)
        copies.append(pltpu.make_async_copy(total.at[:, c], total_hbm.at[:, c], sems.at[n]))
        copies[n].start()
    for copy in copies:
        copy.wait()


def passed_along(block, distance):
    count = lax.axis_size("seq")
    route = [((i - distance) % count, i) for i in range(count)]
    return lax.ppermute(block, "seq", route)


def call(body, name, ins, outs, scratch=()):
    return pl.pallas_call(
        body,
        in_specs=[place for x, place in ins],
        out_specs=[place for shape, kind, place in outs],
        out_shape=[jax.ShapeDtypeStruct(shape, kind) for shape, kind, place in outs],
        scratch_shapes=scratch,
        compiler_params=pltpu.CompilerParams(vmem_limit_bytes=20 << 20),
        cost_estimate=pl.CostEstimate(
            flops=1 << 30, bytes_accessed=4 << 20, transcendentals=0
        ),
        name=name,
    )(*[x for x, place in ins])


def per_device(queries, keys, values, cotangent, neighbour_ids, neighbour_counts):
    dma = pltpu.SemaphoreType.DMA
    pool, tokens, pairs = (ROWS, WIDTH), (GROUP, WIDTH), (ROWS, WIDTH // 2)
    longer = (GROUP, WIDTH + HD)
    q_far = passed_along(queries, 1)
    ids = jnp.transpose(neighbour_ids)
    in_hbm = [
        (pltpu.with_memory_space_constraint(x, pltpu.HBM), HBM)
        for x in (ids, neighbour_counts, queries, cotangent, keys, values)
    ]
    tables = [pltpu.SMEM(ids.shape, jnp.int32), pltpu.SMEM(neighbour_counts.shape, jnp.int32)]
    stats, numer, w_own, q, g, k, v = call(
        own_forward,
        "own_forward",
        in_hbm,
        [
            ((24, HD), F32, VMEM), (tokens, F32, VMEM), (pairs, BF16, VMEM),
            (tokens, BF16, VMEM), (longer, BF16, VMEM), (pool, BF16, VMEM), (pool, BF16, VMEM),
        ],
        tables + [dma((2 + 2 * len(LOADS),))],
    )
    g_far = passed_along(g, 1)
    dp_own, bias_far = call(
        own_dprob,
        "own_dprob",
        in_hbm[:2] + [(g, VMEM), (v, VMEM)],
        [(pairs, BF16, VMEM), ((8, HD), F32, VMEM)],
        tables + [dma((2,))],
    )
    message, w_far, stats_far = call(
        far_forward,
        "far_forward",
        [(x, VMEM) for x in (bias_far, q_far, k, v)],
        [(longer, BF16, VMEM), (pairs, BF16, VMEM), ((16, HD), F32, VMEM)],
    )
    message_back = passed_along(message, -1)
    dq_far, p_far, ds_far = call(
        far_backward,
        "far_backward",
        [(x, VMEM) for x in (g_far, k, v, w_far, message, stats_far)],
        [(tokens, BF16, VMEM), (pairs, BF16, VMEM), (pairs, BF16, VMEM)],
    )
    dq_back = passed_along(dq_far, -1)
    out, dq_own, dk, dv = call(
        gradients,
        "gradients",
        [
            (x, VMEM)
            for x in (
                q, g, q_far, g_far, k, w_own, dp_own, p_far, ds_far, numer, message_back, stats
            )
        ],
        [(tokens, BF16, HBM), (tokens, F32, VMEM), (pool, BF16, HBM), (pool, BF16, HBM)],
        [
            pltpu.VMEM(tokens, BF16), pltpu.VMEM(pool, BF16), pltpu.VMEM(pool, BF16),
            dma((1 + 2 * PAIRS,)),
        ],
    )
    query_grad = call(
        add_queries,
        "add_queries",
        [(dq_own, VMEM), (dq_back, VMEM)],
        [(tokens, BF16, HBM)],
        [pltpu.VMEM(tokens, BF16), dma((2,))],
    )[0]
    return (out, query_grad, dk, dv)


def solution(mesh):
    split = P(("pop", "seq"), None)
    return jax.shard_map(
        per_device,
        mesh=mesh,
        in_specs=(split, split, split, split, P("pop", None), P("pop")),
        out_specs=(split, split, split, split),
        check_vma=False,
    )
```

```python
import math

import jax
import jax.numpy as jnp
from jax import lax
from jax.experimental import pallas as pl
from jax.experimental.pallas import tpu as pltpu
from jax.sharding import PartitionSpec as P

HD = 128
GROUP = 64
NLEN = 128
SLOTS = 8
HELD = 4
WIDTH = 2048
PAIR = 2 * HD
PAIRS = WIDTH // PAIR
ROWS = HELD * NLEN
SCALE = 1.0 / math.sqrt(HD)
TO_LOG2 = SCALE / math.log(2.0)
DEAD = -1e30
LOADS = (0, 2, 5, 8)
BF16 = jnp.bfloat16
F32 = jnp.float32
NT = (((1,), (1,)), ((), ()))
NN = (((1,), (0,)), ((), ()))
TN = (((0,), (0,)), ((), ()))
VMEM = pl.BlockSpec(memory_space=pltpu.VMEM)
HBM = pl.BlockSpec(memory_space=pltpu.HBM)


def dot(a, b, dims):
    return lax.dot_general(a, b, dims, preferred_element_type=F32)


def wide(p):
    return slice(p * PAIR, (p + 1) * PAIR)


def half(p):
    return slice(p * HD, (p + 1) * HD)


def two_heads(x):
    zero = jnp.zeros((GROUP, HD), x.dtype)
    first = jnp.concatenate([x[:, :HD], zero], 1)
    second = jnp.concatenate([zero, x[:, HD:]], 1)
    return jnp.concatenate([first, second], 0)


def own_columns(x):
    return jnp.concatenate([x[:GROUP, :HD], x[GROUP:, HD:]], 1)


def head_sums(x):
    tall = jnp.concatenate([x[:, :HD], x[:, HD:]], 0)
    high = tall.astype(BF16)
    low = (tall - high.astype(F32)).astype(BF16)
    return dot(jnp.ones((16, PAIR), BF16), jnp.concatenate([high, low], 1), NT)[0:1]


def head_sums_by_transpose(x):
    tall = jnp.concatenate([x[:, :HD], x[:, HD:]], 0)
    return jnp.sum(jnp.transpose(tall), axis=0, keepdims=True)


def as_columns(rows):
    empty = jnp.zeros((HD - PAIRS * len(rows), HD), F32)
    return jnp.transpose(jnp.concatenate(rows + [empty], 0))


def spread(columns, p):
    tall = jnp.broadcast_to(columns[:, p : p + 1], (2 * GROUP, HD))
    return jnp.concatenate([tall[:GROUP], tall[GROUP:]], 1)


def live_bias(ids, counts, group, first, n):
    hit = jnp.int32(0)
    for j in range(SLOTS):
        match = (ids[j, group] == first + n) & (j < counts[group])
        hit = hit | match.astype(jnp.int32)
    return jnp.where(hit > 0, F32(0.0), F32(DEAD))


def score_blocks(a, b):
    return [dot(a[n * NLEN : (n + 1) * NLEN], b, NT) for n in range(HELD)]


def softmax_part(raw, bias):
    peaks = [
        jnp.max(raw[n], axis=0, keepdims=True) * TO_LOG2 + bias[n] for n in range(HELD)
    ]
    peak = jnp.maximum(jnp.maximum(peaks[0], peaks[1]), jnp.maximum(peaks[2], peaks[3]))
    e = [
        jnp.exp2(raw[n] * TO_LOG2 - jnp.where(bias[n] < 0.0, F32(-DEAD), peak))
        for n in range(HELD)
    ]
    sums = [jnp.sum(x, axis=0, keepdims=True) for x in e]
    return ([x.astype(BF16) for x in e], peak, (sums[0] + sums[1]) + (sums[2] + sums[3]))


def staggered(stages, lags):
    held = {}
    for t in range(PAIRS + lags[-1]):
        for stage, lag in zip(stages, lags):
            p = t - lag
            if 0 <= p < PAIRS:
                held[p] = stage(p, held.get(p))


def merged(peak_a, total_a, peak_b, total_b):
    top = jnp.maximum(peak_a, peak_b)
    a = jnp.exp2(peak_a - top)
    b = jnp.exp2(peak_b - top)
    inv = 1.0 / (a * total_a + b * total_b)
    return (a * inv, b * inv)


def pieces(x, count):
    out = []
    for _ in range(count - 1):
        out.append(x.astype(BF16).astype(F32))
        x = x - out[-1]
    return out + [x]


def packed(figures):
    tall = []
    for rows, count in figures:
        tall += pieces(rows, count)
    tall += [jnp.zeros((PAIRS, HD), F32)] * (GROUP // PAIRS - len(tall))
    return jnp.concatenate(tall, 0).astype(BF16)


def unpacked(block, counts):
    tall = block.astype(F32)
    out, at = [], 0
    for count in counts:
        x = tall[at : at + PAIRS]
        for n in range(1, count):
            x = x + tall[at + PAIRS * n : at + PAIRS * (n + 1)]
        out.append(x)
        at += PAIRS * count
    return out


def rows_of(n):
    return slice(n * NLEN, (n + 1) * NLEN)


def own_forward(
    ids_hbm, counts_hbm, q_hbm, g_hbm, k_hbm, v_hbm,
    stats, numer, weights, q, g, k, v,
    ids, counts, sems,
):
    copies = [
        pltpu.make_async_copy(ids_hbm, ids, sems.at[0]),
        pltpu.make_async_copy(counts_hbm, counts, sems.at[1]),
        pltpu.make_async_copy(q_hbm, q, sems.at[2]),
        pltpu.make_async_copy(g_hbm, g.at[:, :WIDTH], sems.at[3]),
    ]
    for n in range(len(LOADS) - 1):
        c = slice(LOADS[n] * PAIR, LOADS[n + 1] * PAIR)
        copies.append(pltpu.make_async_copy(k_hbm.at[:, c], k.at[:, c], sems.at[4 + 2 * n]))
        copies.append(pltpu.make_async_copy(v_hbm.at[:, c], v.at[:, c], sems.at[5 + 2 * n]))
    for copy in copies:
        copy.start()
    index = lax.axis_index("seq")
    copies[0].wait()
    copies[1].wait()
    bias = [live_bias(ids, counts, index, index * HELD, n) for n in range(HELD)]
    copies[2].wait()
    copies[3].wait()

    def scores(p, _):
        if p in LOADS:
            n = LOADS.index(p)
            copies[4 + 2 * n].wait()
            copies[5 + 2 * n].wait()
        return score_blocks(k[:, wide(p)], two_heads(q[:, wide(p)]))

    def softmax(p, raw):
        e, peak, total = softmax_part(raw, bias)
        for n in range(HELD):
            weights[rows_of(n), half(p)] = e[n]
        stats[p : p + 1, :] = peak
        stats[8 + p : 9 + p, :] = total
        return e

    def sums(p, e):
        c = wide(p)
        part = own_columns(dot(jnp.concatenate(e, 0), v[:, c], TN))
        numer[:, c] = part
        return part

    def dots(p, part):
        stats[16 + p : 17 + p, :] = head_sums_by_transpose(part * g[:, wide(p)].astype(F32))

    staggered([scores, softmax, sums, dots], (0, 1, 2, 3))
    g[:, WIDTH:] = packed([(stats[:8, :], 3), (stats[8:16, :], 2), (stats[16:, :], 2)])


def own_dprob(ids_hbm, counts_hbm, g, v, dprob, bias_far, ids, counts, sems):
    copies = [
        pltpu.make_async_copy(ids_hbm, ids, sems.at[0]),
        pltpu.make_async_copy(counts_hbm, counts, sems.at[1]),
    ]
    for copy in copies:
        copy.start()
    for p in range(PAIRS):
        c, h = wide(p), half(p)
        blocks = score_blocks(v[:, c], two_heads(g[:, c]))
        for n in range(HELD):
            dprob[rows_of(n), h] = blocks[n].astype(BF16)
    for copy in copies:
        copy.wait()
    index = lax.axis_index("seq")
    before = lax.rem(index + lax.axis_size("seq") - 1, lax.axis_size("seq"))
    for n in range(HELD):
        bias_far[n : n + 1, :] = jnp.full(
            (1, HD), live_bias(ids, counts, before, index * HELD, n), F32
        )
    bias_far[HELD:, :] = jnp.zeros((8 - HELD, HD), F32)


def far_forward(bias_ref, q, k, v, message, weights, stats):
    bias = [bias_ref[n : n + 1, :] for n in range(HELD)]

    def scores(p, _):
        return score_blocks(k[:, wide(p)], two_heads(q[:, wide(p)]))

    def softmax(p, raw):
        e, peak, total = softmax_part(raw, bias)
        for n in range(HELD):
            weights[rows_of(n), half(p)] = e[n]
        stats[p : p + 1, :] = peak
        stats[8 + p : 9 + p, :] = total
        return e

    def sums(p, e):
        part = dot(jnp.concatenate(e, 0), v[:, wide(p)], TN)
        message[:, wide(p)] = own_columns(part).astype(BF16)

    staggered([scores, softmax, sums], (0, 3, 7))
    message[:, WIDTH:] = packed([(stats[:8, :], 3), (stats[8:, :], 2)])


def far_backward(g, k, v, weights, message, stats, dq, prob, dscore):
    peak_own, total_own, dot_own = unpacked(g[:, WIDTH:], (3, 2, 2))
    own, far = merged(peak_own, total_own, stats[0:8, :], stats[8:16, :])
    delta_own = own * dot_own

    def dprobs(p, _):
        gg = g[:, wide(p)]
        dots = head_sums(message[:, wide(p)].astype(F32) * gg.astype(F32))
        delta = delta_own[p : p + 1] + far[p : p + 1] * dots
        return (score_blocks(v[:, wide(p)], two_heads(gg)), delta)

    def dscores(p, held):
        dp, delta = held
        out = []
        for n in range(HELD):
            r, h = rows_of(n), half(p)
            pr = weights[r, h].astype(F32) * far[p : p + 1]
            out.append((pr * (dp[n] - delta)).astype(BF16))
            prob[r, h] = pr.astype(BF16)
            dscore[r, h] = out[n]
        return out

    def dqueries(p, ds):
        part = own_columns(dot(jnp.concatenate(ds, 0), k[:, wide(p)], TN))
        dq[:, wide(p)] = (part * SCALE).astype(BF16)

    staggered([dprobs, dscores, dqueries], (0, 2, 5))


def gradients(
    q, g, q_far, g_far, k, w_own, dp_own, p_far, ds_far, numer, message, stats,
    out_hbm, dq, dk_hbm, dv_hbm,
    out, dk, dv, sems,
):
    peak_far, total_far = unpacked(message[:, WIDTH:], (3, 2))
    own, far = merged(stats[0:8, :], stats[8:16, :], peak_far, total_far)
    factors = as_columns([own, far])
    copies = []
    own_ds = []

    def send(x, to):
        copies.append(pltpu.make_async_copy(x, to, sems.at[len(copies)]))
        copies[-1].start()

    def merge(p, _):
        c = wide(p)
        attended = (
            numer[:, c] * spread(factors, p)
            + message[:, c].astype(F32) * spread(factors, PAIRS + p)
        ).astype(BF16)
        out[:, c] = attended
        if p == PAIRS - 1:
            send(out, out_hbm)
        return head_sums(g[:, c].astype(F32) * attended.astype(F32))

    def dscores(p, delta):
        h = half(p)
        pr = w_own[:, h].astype(F32) * own[p : p + 1]
        ds = (pr * (dp_own[:, h].astype(F32) - delta)).astype(BF16)
        return (pr.astype(BF16), ds)

    def sums(p, held):
        pr, ds = held
        c, h = wide(p), half(p)
        own_ds.append(ds)
        p_all = jnp.concatenate([pr, p_far[:, h]], 1)
        ds_all = jnp.concatenate([ds, ds_far[:, h]], 1)
        g_all = jnp.concatenate([two_heads(g[:, c]), two_heads(g_far[:, c])], 0)
        q_all = jnp.concatenate([two_heads(q[:, c]), two_heads(q_far[:, c])], 0)
        dv_pair = dot(p_all, g_all, NN).astype(BF16)
        dk_pair = (dot(ds_all, q_all, NN) * SCALE).astype(BF16)
        dv[:, c] = dv_pair
        dk[:, c] = dk_pair
        send(dv.at[:, c], dv_hbm.at[:, c])
        send(dk.at[:, c], dk_hbm.at[:, c])

    staggered([merge, dscores, sums], (0, 1, 2))
    for p, ds in enumerate(own_ds):
        dq[:, wide(p)] = own_columns(dot(ds, k[:, wide(p)], TN)) * SCALE
    for copy in copies:
        copy.wait()


def add_queries(own, far, total_hbm, total, sems):
    copies = []
    for n in range(2):
        c = slice(n * WIDTH // 2, (n + 1) * WIDTH // 2)
        total[:, c] = (own[:, c] + far[:, c].astype(F32)).astype(BF16)
        copies.append(pltpu.make_async_copy(total.at[:, c], total_hbm.at[:, c], sems.at[n]))
        copies[n].start()
    for copy in copies:
        copy.wait()


def passed_along(block, distance):
    count = lax.axis_size("seq")
    route = [((i - distance) % count, i) for i in range(count)]
    return lax.ppermute(block, "seq", route)


def call(body, name, ins, outs, scratch=()):
    return pl.pallas_call(
        body,
        in_specs=[place for x, place in ins],
        out_specs=[place for shape, kind, place in outs],
        out_shape=[jax.ShapeDtypeStruct(shape, kind) for shape, kind, place in outs],
        scratch_shapes=scratch,
        compiler_params=pltpu.CompilerParams(vmem_limit_bytes=20 << 20),
        cost_estimate=pl.CostEstimate(
            flops=1 << 30, bytes_accessed=4 << 20, transcendentals=0
        ),
        name=name,
    )(*[x for x, place in ins])


def per_device(queries, keys, values, cotangent, neighbour_ids, neighbour_counts):
    dma = pltpu.SemaphoreType.DMA
    pool, tokens, pairs = (ROWS, WIDTH), (GROUP, WIDTH), (ROWS, WIDTH // 2)
    longer = (GROUP, WIDTH + HD)
    q_far = passed_along(queries, 1)
    ids = jnp.transpose(neighbour_ids)
    in_hbm = [
        (pltpu.with_memory_space_constraint(x, pltpu.HBM), HBM)
        for x in (ids, neighbour_counts, queries, cotangent, keys, values)
    ]
    tables = [pltpu.SMEM(ids.shape, jnp.int32), pltpu.SMEM(neighbour_counts.shape, jnp.int32)]
    stats, numer, w_own, q, g, k, v = call(
        own_forward,
        "own_forward",
        in_hbm,
        [
            ((24, HD), F32, VMEM), (tokens, F32, VMEM), (pairs, BF16, VMEM),
            (tokens, BF16, VMEM), (longer, BF16, VMEM), (pool, BF16, VMEM), (pool, BF16, VMEM),
        ],
        tables + [dma((2 + 2 * len(LOADS),))],
    )
    g_far = passed_along(g, 1)
    dp_own, bias_far = call(
        own_dprob,
        "own_dprob",
        in_hbm[:2] + [(g, VMEM), (v, VMEM)],
        [(pairs, BF16, VMEM), ((8, HD), F32, VMEM)],
        tables + [dma((2,))],
    )
    message, w_far, stats_far = call(
        far_forward,
        "far_forward",
        [(x, VMEM) for x in (bias_far, q_far, k, v)],
        [(longer, BF16, VMEM), (pairs, BF16, VMEM), ((16, HD), F32, VMEM)],
    )
    message_back = passed_along(message, -1)
    dq_far, p_far, ds_far = call(
        far_backward,
        "far_backward",
        [(x, VMEM) for x in (g_far, k, v, w_far, message, stats_far)],
        [(tokens, BF16, VMEM), (pairs, BF16, VMEM), (pairs, BF16, VMEM)],
    )
    dq_back = passed_along(dq_far, -1)
    out, dq_own, dk, dv = call(
        gradients,
        "gradients",
        [
            (x, VMEM)
            for x in (
                q, g, q_far, g_far, k, w_own, dp_own, p_far, ds_far, numer, message_back, stats
            )
        ],
        [(tokens, BF16, HBM), (tokens, F32, VMEM), (pool, BF16, HBM), (pool, BF16, HBM)],
        [
            pltpu.VMEM(tokens, BF16), pltpu.VMEM(pool, BF16), pltpu.VMEM(pool, BF16),
            dma((1 + 2 * PAIRS,)),
        ],
    )
    query_grad = call(
        add_queries,
        "add_queries",
        [(dq_own, VMEM), (dq_back, VMEM)],
        [(tokens, BF16, HBM)],
        [pltpu.VMEM(tokens, BF16), dma((2,))],
    )[0]
    return (out, query_grad, dk, dv)


def solution(mesh):
    split = P(("pop", "seq"), None)
    return jax.shard_map(
        per_device,
        mesh=mesh,
        in_specs=(split, split, split, split, P("pop", None), P("pop")),
        out_specs=(split, split, split, split),
        check_vma=False,
    )
```

```python
import math

import jax
import jax.numpy as jnp
from jax import lax
from jax.experimental import pallas as pl
from jax.experimental.pallas import tpu as pltpu
from jax.sharding import PartitionSpec as P

HD = 128
GROUP = 64
NLEN = 128
SLOTS = 8
HELD = 4
WIDTH = 2048
PAIR = 2 * HD
PAIRS = WIDTH // PAIR
ROWS = HELD * NLEN
SCALE = 1.0 / math.sqrt(HD)
TO_LOG2 = SCALE / math.log(2.0)
DEAD = -1e30
LOADS = (0, 2, 5, 8)
BF16 = jnp.bfloat16
F32 = jnp.float32
NT = (((1,), (1,)), ((), ()))
NN = (((1,), (0,)), ((), ()))
TN = (((0,), (0,)), ((), ()))
VMEM = pl.BlockSpec(memory_space=pltpu.VMEM)
HBM = pl.BlockSpec(memory_space=pltpu.HBM)


def dot(a, b, dims):
    return lax.dot_general(a, b, dims, preferred_element_type=F32)


def wide(p):
    return slice(p * PAIR, (p + 1) * PAIR)


def half(p):
    return slice(p * HD, (p + 1) * HD)


def two_heads(x):
    zero = jnp.zeros((GROUP, HD), x.dtype)
    first = jnp.concatenate([x[:, :HD], zero], 1)
    second = jnp.concatenate([zero, x[:, HD:]], 1)
    return jnp.concatenate([first, second], 0)


def own_columns(x):
    return jnp.concatenate([x[:GROUP, :HD], x[GROUP:, HD:]], 1)


def head_sums(x):
    tall = jnp.concatenate([x[:, :HD], x[:, HD:]], 0)
    high = tall.astype(BF16)
    low = (tall - high.astype(F32)).astype(BF16)
    return dot(jnp.ones((16, PAIR), BF16), jnp.concatenate([high, low], 1), NT)[0:1]


def head_sums_by_transpose(x):
    tall = jnp.concatenate([x[:, :HD], x[:, HD:]], 0)
    return jnp.sum(jnp.transpose(tall), axis=0, keepdims=True)


def as_columns(rows):
    empty = jnp.zeros((HD - PAIRS * len(rows), HD), F32)
    return jnp.transpose(jnp.concatenate(rows + [empty], 0))


def spread(columns, p):
    tall = jnp.broadcast_to(columns[:, p : p + 1], (2 * GROUP, HD))
    return jnp.concatenate([tall[:GROUP], tall[GROUP:]], 1)


def live_bias(ids, counts, group, first, n):
    hit = jnp.int32(0)
    for j in range(SLOTS):
        match = (ids[j, group] == first + n) & (j < counts[group])
        hit = hit | match.astype(jnp.int32)
    return jnp.where(hit > 0, F32(0.0), F32(DEAD))


def score_blocks(a, b):
    return [dot(a[n * NLEN : (n + 1) * NLEN], b, NT) for n in range(HELD)]


def softmax_part(raw, bias):
    peaks = [
        jnp.max(raw[n], axis=0, keepdims=True) * TO_LOG2 + bias[n] for n in range(HELD)
    ]
    peak = jnp.maximum(jnp.maximum(peaks[0], peaks[1]), jnp.maximum(peaks[2], peaks[3]))
    e = [
        jnp.exp2(raw[n] * TO_LOG2 - jnp.where(bias[n] < 0.0, F32(-DEAD), peak))
        for n in range(HELD)
    ]
    sums = [jnp.sum(x, axis=0, keepdims=True) for x in e]
    return ([x.astype(BF16) for x in e], peak, (sums[0] + sums[1]) + (sums[2] + sums[3]))


def staggered(stages, lags):
    held = {}
    for t in range(PAIRS + lags[-1]):
        for stage, lag in zip(stages, lags):
            p = t - lag
            if 0 <= p < PAIRS:
                held[p] = stage(p, held.get(p))


def merged(peak_a, total_a, peak_b, total_b):
    top = jnp.maximum(peak_a, peak_b)
    a = jnp.exp2(peak_a - top)
    b = jnp.exp2(peak_b - top)
    inv = 1.0 / (a * total_a + b * total_b)
    return (a * inv, b * inv)


def pieces(x, count):
    out = []
    for _ in range(count - 1):
        out.append(x.astype(BF16).astype(F32))
        x = x - out[-1]
    return out + [x]


def packed(figures):
    tall = []
    for rows, count in figures:
        tall += pieces(rows, count)
    tall += [jnp.zeros((PAIRS, HD), F32)] * (GROUP // PAIRS - len(tall))
    return jnp.concatenate(tall, 0).astype(BF16)


def unpacked(block, counts):
    tall = block.astype(F32)
    out, at = [], 0
    for count in counts:
        x = tall[at : at + PAIRS]
        for n in range(1, count):
            x = x + tall[at + PAIRS * n : at + PAIRS * (n + 1)]
        out.append(x)
        at += PAIRS * count
    return out


def rows_of(n):
    return slice(n * NLEN, (n + 1) * NLEN)


def own_forward(
    ids_hbm, counts_hbm, q_hbm, g_hbm, k_hbm, v_hbm,
    stats, numer, weights, q, g, k, v,
    ids, counts, sems,
):
    copies = [
        pltpu.make_async_copy(ids_hbm, ids, sems.at[0]),
        pltpu.make_async_copy(counts_hbm, counts, sems.at[1]),
        pltpu.make_async_copy(q_hbm, q, sems.at[2]),
        pltpu.make_async_copy(g_hbm, g.at[:, :WIDTH], sems.at[3]),
    ]
    for n in range(len(LOADS) - 1):
        c = slice(LOADS[n] * PAIR, LOADS[n + 1] * PAIR)
        copies.append(pltpu.make_async_copy(k_hbm.at[:, c], k.at[:, c], sems.at[4 + 2 * n]))
        copies.append(pltpu.make_async_copy(v_hbm.at[:, c], v.at[:, c], sems.at[5 + 2 * n]))
    for copy in copies:
        copy.start()
    index = lax.axis_index("seq")
    copies[0].wait()
    copies[1].wait()
    bias = [live_bias(ids, counts, index, index * HELD, n) for n in range(HELD)]
    copies[2].wait()
    copies[3].wait()

    def scores(p, _):
        if p in LOADS:
            n = LOADS.index(p)
            copies[4 + 2 * n].wait()
            copies[5 + 2 * n].wait()
        return score_blocks(k[:, wide(p)], two_heads(q[:, wide(p)]))

    def softmax(p, raw):
        e, peak, total = softmax_part(raw, bias)
        for n in range(HELD):
            weights[rows_of(n), half(p)] = e[n]
        stats[p : p + 1, :] = peak
        stats[8 + p : 9 + p, :] = total
        return e

    def sums(p, e):
        c = wide(p)
        part = own_columns(dot(jnp.concatenate(e, 0), v[:, c], TN))
        numer[:, c] = part
        return part

    def dots(p, part):
        stats[16 + p : 17 + p, :] = head_sums_by_transpose(part * g[:, wide(p)].astype(F32))

    staggered([scores, softmax, sums, dots], (0, 1, 2, 3))
    g[:, WIDTH:] = packed([(stats[:8, :], 3), (stats[8:16, :], 2), (stats[16:, :], 2)])


def own_dprob(ids_hbm, counts_hbm, g, v, dprob, bias_far, ids, counts, sems):
    copies = [
        pltpu.make_async_copy(ids_hbm, ids, sems.at[0]),
        pltpu.make_async_copy(counts_hbm, counts, sems.at[1]),
    ]
    for copy in copies:
        copy.start()
    for p in range(PAIRS):
        c, h = wide(p), half(p)
        blocks = score_blocks(v[:, c], two_heads(g[:, c]))
        for n in range(HELD):
            dprob[rows_of(n), h] = blocks[n].astype(BF16)
    for copy in copies:
        copy.wait()
    index = lax.axis_index("seq")
    before = lax.rem(index + lax.axis_size("seq") - 1, lax.axis_size("seq"))
    for n in range(HELD):
        bias_far[n : n + 1, :] = jnp.full(
            (1, HD), live_bias(ids, counts, before, index * HELD, n), F32
        )
    bias_far[HELD:, :] = jnp.zeros((8 - HELD, HD), F32)


def far_forward(bias_ref, q, k, v, message, weights, stats):
    bias = [bias_ref[n : n + 1, :] for n in range(HELD)]

    def scores(p, _):
        return score_blocks(k[:, wide(p)], two_heads(q[:, wide(p)]))

    def softmax(p, raw):
        e, peak, total = softmax_part(raw, bias)
        for n in range(HELD):
            weights[rows_of(n), half(p)] = e[n]
        stats[p : p + 1, :] = peak
        stats[8 + p : 9 + p, :] = total
        return e

    def sums(p, e):
        part = dot(jnp.concatenate(e, 0), v[:, wide(p)], TN)
        message[:, wide(p)] = own_columns(part).astype(BF16)

    staggered([scores, softmax, sums], (0, 3, 7))
    message[:, WIDTH:] = packed([(stats[:8, :], 3), (stats[8:, :], 2)])


def far_backward(g, k, v, weights, message, stats, dq, dscore, factor):
    peak_own, total_own, dot_own = unpacked(g[:, WIDTH:], (3, 2, 2))
    own, far = merged(peak_own, total_own, stats[0:8, :], stats[8:16, :])
    delta_own = own * dot_own
    factor[...] = far

    def dprobs(p, _):
        gg = g[:, wide(p)]
        dots = head_sums(message[:, wide(p)].astype(F32) * gg.astype(F32))
        delta = delta_own[p : p + 1] + far[p : p + 1] * dots
        return (score_blocks(v[:, wide(p)], two_heads(gg)), delta)

    def dscores(p, held):
        dp, delta = held
        out = []
        for n in range(HELD):
            r, h = rows_of(n), half(p)
            pr = weights[r, h].astype(F32) * far[p : p + 1]
            out.append((pr * (dp[n] - delta)).astype(BF16))
            dscore[r, h] = out[n]
        return out

    def dqueries(p, ds):
        part = own_columns(dot(jnp.concatenate(ds, 0), k[:, wide(p)], TN))
        dq[:, wide(p)] = (part * SCALE).astype(BF16)

    staggered([dprobs, dscores, dqueries], (0, 2, 5))


def gradients(
    q, g, q_far, g_far, k, w_own, dp_own, w_far, ds_far, f_far, numer, message, stats,
    out_hbm, dq, dk_hbm, dv_hbm,
    out, dk, dv, sems,
):
    peak_far, total_far = unpacked(message[:, WIDTH:], (3, 2))
    own, far = merged(stats[0:8, :], stats[8:16, :], peak_far, total_far)
    factors = as_columns([own, far])
    copies = []
    own_ds = []

    def send(x, to):
        copies.append(pltpu.make_async_copy(x, to, sems.at[len(copies)]))
        copies[-1].start()

    def merge(p, _):
        c = wide(p)
        attended = (
            numer[:, c] * spread(factors, p)
            + message[:, c].astype(F32) * spread(factors, PAIRS + p)
        ).astype(BF16)
        out[:, c] = attended
        if p == PAIRS - 1:
            send(out, out_hbm)
        return head_sums(g[:, c].astype(F32) * attended.astype(F32))

    def dscores(p, delta):
        h = half(p)
        pr = w_own[:, h].astype(F32) * own[p : p + 1]
        ds = (pr * (dp_own[:, h].astype(F32) - delta)).astype(BF16)
        return (pr.astype(BF16), ds)

    def sums(p, held):
        pr, ds = held
        c, h = wide(p), half(p)
        own_ds.append(ds)
        pr_far = (w_far[:, h].astype(F32) * f_far[p : p + 1, :]).astype(BF16)
        p_all = jnp.concatenate([pr, pr_far], 1)
        ds_all = jnp.concatenate([ds, ds_far[:, h]], 1)
        g_all = jnp.concatenate([two_heads(g[:, c]), two_heads(g_far[:, c])], 0)
        q_all = jnp.concatenate([two_heads(q[:, c]), two_heads(q_far[:, c])], 0)
        dv_pair = dot(p_all, g_all, NN).astype(BF16)
        dk_pair = (dot(ds_all, q_all, NN) * SCALE).astype(BF16)
        dv[:, c] = dv_pair
        dk[:, c] = dk_pair
        send(dv.at[:, c], dv_hbm.at[:, c])
        send(dk.at[:, c], dk_hbm.at[:, c])

    staggered([merge, dscores, sums], (0, 1, 2))
    for p, ds in enumerate(own_ds):
        dq[:, wide(p)] = own_columns(dot(ds, k[:, wide(p)], TN)) * SCALE
    for copy in copies:
        copy.wait()


def add_queries(own, far, total_hbm, total, sems):
    copies = []
    for n in range(2):
        c = slice(n * WIDTH // 2, (n + 1) * WIDTH // 2)
        total[:, c] = (own[:, c] + far[:, c].astype(F32)).astype(BF16)
        copies.append(pltpu.make_async_copy(total.at[:, c], total_hbm.at[:, c], sems.at[n]))
        copies[n].start()
    for copy in copies:
        copy.wait()


def passed_along(block, distance):
    count = lax.axis_size("seq")
    route = [((i - distance) % count, i) for i in range(count)]
    return lax.ppermute(block, "seq", route)


def call(body, name, ins, outs, scratch=()):
    return pl.pallas_call(
        body,
        in_specs=[place for x, place in ins],
        out_specs=[place for shape, kind, place in outs],
        out_shape=[jax.ShapeDtypeStruct(shape, kind) for shape, kind, place in outs],
        scratch_shapes=scratch,
        compiler_params=pltpu.CompilerParams(vmem_limit_bytes=20 << 20),
        cost_estimate=pl.CostEstimate(
            flops=1 << 30, bytes_accessed=4 << 20, transcendentals=0
        ),
        name=name,
    )(*[x for x, place in ins])


def per_device(queries, keys, values, cotangent, neighbour_ids, neighbour_counts):
    dma = pltpu.SemaphoreType.DMA
    pool, tokens, pairs = (ROWS, WIDTH), (GROUP, WIDTH), (ROWS, WIDTH // 2)
    longer = (GROUP, WIDTH + HD)
    q_far = passed_along(queries, 1)
    ids = jnp.transpose(neighbour_ids)
    in_hbm = [
        (pltpu.with_memory_space_constraint(x, pltpu.HBM), HBM)
        for x in (ids, neighbour_counts, queries, cotangent, keys, values)
    ]
    tables = [pltpu.SMEM(ids.shape, jnp.int32), pltpu.SMEM(neighbour_counts.shape, jnp.int32)]
    stats, numer, w_own, q, g, k, v = call(
        own_forward,
        "own_forward",
        in_hbm,
        [
            ((24, HD), F32, VMEM), (tokens, F32, VMEM), (pairs, BF16, VMEM),
            (tokens, BF16, VMEM), (longer, BF16, VMEM), (pool, BF16, VMEM), (pool, BF16, VMEM),
        ],
        tables + [dma((2 + 2 * len(LOADS),))],
    )
    g_far = passed_along(g, 1)
    dp_own, bias_far = call(
        own_dprob,
        "own_dprob",
        in_hbm[:2] + [(g, VMEM), (v, VMEM)],
        [(pairs, BF16, VMEM), ((8, HD), F32, VMEM)],
        tables + [dma((2,))],
    )
    message, w_far, stats_far = call(
        far_forward,
        "far_forward",
        [(x, VMEM) for x in (bias_far, q_far, k, v)],
        [(longer, BF16, VMEM), (pairs, BF16, VMEM), ((16, HD), F32, VMEM)],
    )
    message_back = passed_along(message, -1)
    dq_far, ds_far, f_far = call(
        far_backward,
        "far_backward",
        [(x, VMEM) for x in (g_far, k, v, w_far, message, stats_far)],
        [(tokens, BF16, VMEM), (pairs, BF16, VMEM), ((8, HD), F32, VMEM)],
    )
    dq_back = passed_along(dq_far, -1)
    out, dq_own, dk, dv = call(
        gradients,
        "gradients",
        [
            (x, VMEM)
            for x in (
                q, g, q_far, g_far, k, w_own, dp_own, w_far, ds_far, f_far, numer, message_back, stats
            )
        ],
        [(tokens, BF16, HBM), (tokens, F32, VMEM), (pool, BF16, HBM), (pool, BF16, HBM)],
        [
            pltpu.VMEM(tokens, BF16), pltpu.VMEM(pool, BF16), pltpu.VMEM(pool, BF16),
            dma((1 + 2 * PAIRS,)),
        ],
    )
    query_grad = call(
        add_queries,
        "add_queries",
        [(dq_own, VMEM), (dq_back, VMEM)],
        [(tokens, BF16, HBM)],
        [pltpu.VMEM(tokens, BF16), dma((2,))],
    )[0]
    return (out, query_grad, dk, dv)


def solution(mesh):
    split = P(("pop", "seq"), None)
    return jax.shard_map(
        per_device,
        mesh=mesh,
        in_specs=(split, split, split, split, P("pop", None), P("pop")),
        out_specs=(split, split, split, split),
        check_vma=False,
    )
```

```python
import math

import jax
import jax.numpy as jnp
from jax import lax
from jax.experimental import pallas as pl
from jax.experimental.pallas import tpu as pltpu
from jax.sharding import PartitionSpec as P

HD = 128
GROUP = 64
NLEN = 128
SLOTS = 8
HELD = 4
WIDTH = 2048
PAIR = 2 * HD
PAIRS = WIDTH // PAIR
ROWS = HELD * NLEN
SCALE = 1.0 / math.sqrt(HD)
TO_LOG2 = SCALE / math.log(2.0)
DEAD = -1e30
LOADS = (0, 2, 5, 8)
BF16 = jnp.bfloat16
F32 = jnp.float32
NT = (((1,), (1,)), ((), ()))
NN = (((1,), (0,)), ((), ()))
TN = (((0,), (0,)), ((), ()))
VMEM = pl.BlockSpec(memory_space=pltpu.VMEM)
HBM = pl.BlockSpec(memory_space=pltpu.HBM)


def dot(a, b, dims):
    return lax.dot_general(a, b, dims, preferred_element_type=F32)


def wide(p):
    return slice(p * PAIR, (p + 1) * PAIR)


def half(p):
    return slice(p * HD, (p + 1) * HD)


def two_heads(x):
    zero = jnp.zeros((GROUP, HD), x.dtype)
    first = jnp.concatenate([x[:, :HD], zero], 1)
    second = jnp.concatenate([zero, x[:, HD:]], 1)
    return jnp.concatenate([first, second], 0)


def own_columns(x):
    return jnp.concatenate([x[:GROUP, :HD], x[GROUP:, HD:]], 1)


def head_sums(x):
    tall = jnp.concatenate([x[:, :HD], x[:, HD:]], 0)
    high = tall.astype(BF16)
    low = (tall - high.astype(F32)).astype(BF16)
    return dot(jnp.ones((16, PAIR), BF16), jnp.concatenate([high, low], 1), NT)[0:1]


def head_sums_by_transpose(x):
    tall = jnp.concatenate([x[:, :HD], x[:, HD:]], 0)
    return jnp.sum(jnp.transpose(tall), axis=0, keepdims=True)


def as_columns(rows):
    empty = jnp.zeros((HD - PAIRS * len(rows), HD), F32)
    return jnp.transpose(jnp.concatenate(rows + [empty], 0))


def spread(columns, p):
    tall = jnp.broadcast_to(columns[:, p : p + 1], (2 * GROUP, HD))
    return jnp.concatenate([tall[:GROUP], tall[GROUP:]], 1)


def live_bias(ids, counts, group, first, n):
    hit = jnp.int32(0)
    for j in range(SLOTS):
        match = (ids[j, group] == first + n) & (j < counts[group])
        hit = hit | match.astype(jnp.int32)
    return jnp.where(hit > 0, F32(0.0), F32(DEAD))


def score_blocks(a, b):
    return [dot(a[n * NLEN : (n + 1) * NLEN], b, NT) for n in range(HELD)]


def softmax_part(raw, bias):
    peaks = [
        jnp.max(raw[n], axis=0, keepdims=True) * TO_LOG2 + bias[n] for n in range(HELD)
    ]
    peak = jnp.maximum(jnp.maximum(peaks[0], peaks[1]), jnp.maximum(peaks[2], peaks[3]))
    e = [
        jnp.exp2(raw[n] * TO_LOG2 - jnp.where(bias[n] < 0.0, F32(-DEAD), peak))
        for n in range(HELD)
    ]
    sums = [jnp.sum(x, axis=0, keepdims=True) for x in e]
    return ([x.astype(BF16) for x in e], peak, (sums[0] + sums[1]) + (sums[2] + sums[3]))


def staggered(stages, lags):
    held = {}
    for t in range(PAIRS + lags[-1]):
        for stage, lag in zip(stages, lags):
            p = t - lag
            if 0 <= p < PAIRS:
                held[p] = stage(p, held.get(p))


def merged(peak_a, total_a, peak_b, total_b):
    top = jnp.maximum(peak_a, peak_b)
    a = jnp.exp2(peak_a - top)
    b = jnp.exp2(peak_b - top)
    inv = 1.0 / (a * total_a + b * total_b)
    return (a * inv, b * inv)


def pieces(x, count):
    out = []
    for _ in range(count - 1):
        out.append(x.astype(BF16).astype(F32))
        x = x - out[-1]
    return out + [x]


def packed(figures):
    tall = []
    for rows, count in figures:
        tall += pieces(rows, count)
    tall += [jnp.zeros((PAIRS, HD), F32)] * (GROUP // PAIRS - len(tall))
    return jnp.concatenate(tall, 0).astype(BF16)


def unpacked(block, counts):
    tall = block.astype(F32)
    out, at = [], 0
    for count in counts:
        x = tall[at : at + PAIRS]
        for n in range(1, count):
            x = x + tall[at + PAIRS * n : at + PAIRS * (n + 1)]
        out.append(x)
        at += PAIRS * count
    return out


def rows_of(n):
    return slice(n * NLEN, (n + 1) * NLEN)


def own_forward(
    ids_hbm, counts_hbm, q_hbm, g_hbm, k_hbm, v_hbm,
    stats, numer, weights, q, g, k, v,
    ids, counts, sems,
):
    copies = [
        pltpu.make_async_copy(ids_hbm, ids, sems.at[0]),
        pltpu.make_async_copy(counts_hbm, counts, sems.at[1]),
        pltpu.make_async_copy(q_hbm, q, sems.at[2]),
        pltpu.make_async_copy(g_hbm, g.at[:, :WIDTH], sems.at[3]),
    ]
    for n in range(len(LOADS) - 1):
        c = slice(LOADS[n] * PAIR, LOADS[n + 1] * PAIR)
        copies.append(pltpu.make_async_copy(k_hbm.at[:, c], k.at[:, c], sems.at[4 + 2 * n]))
        copies.append(pltpu.make_async_copy(v_hbm.at[:, c], v.at[:, c], sems.at[5 + 2 * n]))
    for copy in copies:
        copy.start()
    index = lax.axis_index("seq")
    copies[0].wait()
    copies[1].wait()
    bias = [live_bias(ids, counts, index, index * HELD, n) for n in range(HELD)]
    copies[2].wait()
    copies[3].wait()

    def scores(p, _):
        if p in LOADS:
            n = LOADS.index(p)
            copies[4 + 2 * n].wait()
            copies[5 + 2 * n].wait()
        return score_blocks(k[:, wide(p)], two_heads(q[:, wide(p)]))

    def softmax(p, raw):
        e, peak, total = softmax_part(raw, bias)
        for n in range(HELD):
            weights[rows_of(n), half(p)] = e[n]
        stats[p : p + 1, :] = peak
        stats[8 + p : 9 + p, :] = total
        return e

    def sums(p, e):
        c = wide(p)
        part = own_columns(dot(jnp.concatenate(e, 0), v[:, c], TN))
        numer[:, c] = part
        return part

    def dots(p, part):
        stats[16 + p : 17 + p, :] = head_sums_by_transpose(part * g[:, wide(p)].astype(F32))

    staggered([scores, softmax, sums, dots], (0, 1, 2, 3))
    g[:, WIDTH:] = packed([(stats[:8, :], 3), (stats[8:16, :], 2), (stats[16:, :], 2)])


def own_dprob(ids_hbm, counts_hbm, g, v, dprob, bias_far, ids, counts, sems):
    copies = [
        pltpu.make_async_copy(ids_hbm, ids, sems.at[0]),
        pltpu.make_async_copy(counts_hbm, counts, sems.at[1]),
    ]
    for copy in copies:
        copy.start()
    for p in range(PAIRS):
        c, h = wide(p), half(p)
        blocks = score_blocks(v[:, c], two_heads(g[:, c]))
        for n in range(HELD):
            dprob[rows_of(n), h] = blocks[n].astype(BF16)
    for copy in copies:
        copy.wait()
    index = lax.axis_index("seq")
    before = lax.rem(index + lax.axis_size("seq") - 1, lax.axis_size("seq"))
    for n in range(HELD):
        bias_far[n : n + 1, :] = jnp.full(
            (1, HD), live_bias(ids, counts, before, index * HELD, n), F32
        )
    bias_far[HELD:, :] = jnp.zeros((8 - HELD, HD), F32)


def far_forward(bias_ref, q, k, v, message, weights, stats):
    bias = [bias_ref[n : n + 1, :] for n in range(HELD)]

    def scores(p, _):
        return score_blocks(k[:, wide(p)], two_heads(q[:, wide(p)]))

    def softmax(p, raw):
        e, peak, total = softmax_part(raw, bias)
        for n in range(HELD):
            weights[rows_of(n), half(p)] = e[n]
        stats[p : p + 1, :] = peak
        stats[8 + p : 9 + p, :] = total
        return e

    def sums(p, e):
        part = dot(jnp.concatenate(e, 0), v[:, wide(p)], TN)
        message[:, wide(p)] = own_columns(part).astype(BF16)

    staggered([scores, softmax, sums], (0, 3, 7))
    message[:, WIDTH:] = packed([(stats[:8, :], 3), (stats[8:, :], 2)])


def far_backward(g, k, v, weights, message, stats, dq, dscore, factor):
    peak_own, total_own, dot_own = unpacked(g[:, WIDTH:], (3, 2, 2))
    own, far = merged(peak_own, total_own, stats[0:8, :], stats[8:16, :])
    delta_own = own * dot_own
    factor[...] = far

    def dprobs(p, _):
        gg = g[:, wide(p)]
        dots = head_sums(message[:, wide(p)].astype(F32) * gg.astype(F32))
        delta = delta_own[p : p + 1] + far[p : p + 1] * dots
        return (score_blocks(v[:, wide(p)], two_heads(gg)), delta)

    def dscores(p, held):
        dp, delta = held
        out = []
        for n in range(HELD):
            r, h = rows_of(n), half(p)
            pr = weights[r, h].astype(F32) * far[p : p + 1]
            out.append((pr * (dp[n] - delta)).astype(BF16))
            dscore[r, h] = out[n]
        return out

    def dqueries(p, ds):
        part = own_columns(dot(jnp.concatenate(ds, 0), k[:, wide(p)], TN))
        dq[:, wide(p)] = (part * SCALE).astype(BF16)

    staggered([dprobs, dscores, dqueries], (0, 3, 6))


def gradients(
    q, g, q_far, g_far, k, w_own, dp_own, w_far, ds_far, f_far, numer, message, stats,
    out_hbm, dq, dk_hbm, dv_hbm,
    out, dk, dv, sems,
):
    peak_far, total_far = unpacked(message[:, WIDTH:], (3, 2))
    own, far = merged(stats[0:8, :], stats[8:16, :], peak_far, total_far)
    factors = as_columns([own, far])
    copies = []
    own_ds = []

    def send(x, to):
        copies.append(pltpu.make_async_copy(x, to, sems.at[len(copies)]))
        copies[-1].start()

    def merge(p, _):
        c = wide(p)
        attended = (
            numer[:, c] * spread(factors, p)
            + message[:, c].astype(F32) * spread(factors, PAIRS + p)
        ).astype(BF16)
        out[:, c] = attended
        if p == PAIRS - 1:
            send(out, out_hbm)
        return head_sums(g[:, c].astype(F32) * attended.astype(F32))

    def dscores(p, delta):
        h = half(p)
        pr = w_own[:, h].astype(F32) * own[p : p + 1]
        ds = (pr * (dp_own[:, h].astype(F32) - delta)).astype(BF16)
        return (pr.astype(BF16), ds)

    def sums(p, held):
        pr, ds = held
        c, h = wide(p), half(p)
        own_ds.append(ds)
        pr_far = (w_far[:, h].astype(F32) * f_far[p : p + 1, :]).astype(BF16)
        p_all = jnp.concatenate([pr, pr_far], 1)
        ds_all = jnp.concatenate([ds, ds_far[:, h]], 1)
        g_all = jnp.concatenate([two_heads(g[:, c]), two_heads(g_far[:, c])], 0)
        q_all = jnp.concatenate([two_heads(q[:, c]), two_heads(q_far[:, c])], 0)
        dv_pair = dot(p_all, g_all, NN).astype(BF16)
        dk_pair = (dot(ds_all, q_all, NN) * SCALE).astype(BF16)
        dv[:, c] = dv_pair
        dk[:, c] = dk_pair
        send(dv.at[:, c], dv_hbm.at[:, c])
        send(dk.at[:, c], dk_hbm.at[:, c])

    staggered([merge, dscores, sums], (0, 1, 2))
    for p, ds in enumerate(own_ds):
        dq[:, wide(p)] = own_columns(dot(ds, k[:, wide(p)], TN)) * SCALE
    for copy in copies:
        copy.wait()


def add_queries(own, far, total_hbm, total, sems):
    copies = []
    for n in range(2):
        c = slice(n * WIDTH // 2, (n + 1) * WIDTH // 2)
        total[:, c] = (own[:, c] + far[:, c].astype(F32)).astype(BF16)
        copies.append(pltpu.make_async_copy(total.at[:, c], total_hbm.at[:, c], sems.at[n]))
        copies[n].start()
    for copy in copies:
        copy.wait()


def passed_along(block, distance):
    count = lax.axis_size("seq")
    route = [((i - distance) % count, i) for i in range(count)]
    return lax.ppermute(block, "seq", route)


def call(body, name, ins, outs, scratch=()):
    return pl.pallas_call(
        body,
        in_specs=[place for x, place in ins],
        out_specs=[place for shape, kind, place in outs],
        out_shape=[jax.ShapeDtypeStruct(shape, kind) for shape, kind, place in outs],
        scratch_shapes=scratch,
        compiler_params=pltpu.CompilerParams(vmem_limit_bytes=20 << 20),
        cost_estimate=pl.CostEstimate(
            flops=1 << 30, bytes_accessed=4 << 20, transcendentals=0
        ),
        name=name,
    )(*[x for x, place in ins])


def per_device(queries, keys, values, cotangent, neighbour_ids, neighbour_counts):
    dma = pltpu.SemaphoreType.DMA
    pool, tokens, pairs = (ROWS, WIDTH), (GROUP, WIDTH), (ROWS, WIDTH // 2)
    longer = (GROUP, WIDTH + HD)
    q_far = passed_along(queries, 1)
    ids = jnp.transpose(neighbour_ids)
    in_hbm = [
        (pltpu.with_memory_space_constraint(x, pltpu.HBM), HBM)
        for x in (ids, neighbour_counts, queries, cotangent, keys, values)
    ]
    tables = [pltpu.SMEM(ids.shape, jnp.int32), pltpu.SMEM(neighbour_counts.shape, jnp.int32)]
    stats, numer, w_own, q, g, k, v = call(
        own_forward,
        "own_forward",
        in_hbm,
        [
            ((24, HD), F32, VMEM), (tokens, F32, VMEM), (pairs, BF16, VMEM),
            (tokens, BF16, VMEM), (longer, BF16, VMEM), (pool, BF16, VMEM), (pool, BF16, VMEM),
        ],
        tables + [dma((2 + 2 * len(LOADS),))],
    )
    g_far = passed_along(g, 1)
    dp_own, bias_far = call(
        own_dprob,
        "own_dprob",
        in_hbm[:2] + [(g, VMEM), (v, VMEM)],
        [(pairs, BF16, VMEM), ((8, HD), F32, VMEM)],
        tables + [dma((2,))],
    )
    message, w_far, stats_far = call(
        far_forward,
        "far_forward",
        [(x, VMEM) for x in (bias_far, q_far, k, v)],
        [(longer, BF16, VMEM), (pairs, BF16, VMEM), ((16, HD), F32, VMEM)],
    )
    message_back = passed_along(message, -1)
    dq_far, ds_far, f_far = call(
        far_backward,
        "far_backward",
        [(x, VMEM) for x in (g_far, k, v, w_far, message, stats_far)],
        [(tokens, BF16, VMEM), (pairs, BF16, VMEM), ((8, HD), F32, VMEM)],
    )
    dq_back = passed_along(dq_far, -1)
    out, dq_own, dk, dv = call(
        gradients,
        "gradients",
        [
            (x, VMEM)
            for x in (
                q, g, q_far, g_far, k, w_own, dp_own, w_far, ds_far, f_far, numer, message_back, stats
            )
        ],
        [(tokens, BF16, HBM), (tokens, F32, VMEM), (pool, BF16, HBM), (pool, BF16, HBM)],
        [
            pltpu.VMEM(tokens, BF16), pltpu.VMEM(pool, BF16), pltpu.VMEM(pool, BF16),
            dma((1 + 2 * PAIRS,)),
        ],
    )
    query_grad = call(
        add_queries,
        "add_queries",
        [(dq_own, VMEM), (dq_back, VMEM)],
        [(tokens, BF16, HBM)],
        [pltpu.VMEM(tokens, BF16), dma((2,))],
    )[0]
    return (out, query_grad, dk, dv)


def solution(mesh):
    split = P(("pop", "seq"), None)
    return jax.shard_map(
        per_device,
        mesh=mesh,
        in_specs=(split, split, split, split, P("pop", None), P("pop")),
        out_specs=(split, split, split, split),
        check_vma=False,
    )
```
